128 devices in a mesh: dp: 32 (over z, y_lo, x), cls: 4 (over y_hi, core).
Axes of the slice: x: 4, y: 4 (y_hi: 2, y_lo: 2; y = y_hi * 2 + y_lo), z: 4, core: 2. Of those that a mesh axis runs over, the one named last changes fastest.
Arguments:
- particles: bfloat16 [256, 2, 288, 128], P('dp'), may hold values from -20 to 20
- references: bfloat16 [288, 2, 200, 128], P('dp', None, 'cls'), may hold values from -9 to 9
- ctf_table: float32 [16, 128], replicated, may hold values from -0.1 to 0.1
- rot_offset: int32 [200], P('cls'), may hold values from 0 to 7
- prior_shift: int32 [256, 2], P('dp'), may hold values from -8 to 8
- defocus_group: int32 [256], P('dp'), may hold values from 0 to 15
Outputs:
- log_evidence: float32 [256], P('dp')
- class_posterior: float32 [256, 200], P('dp', 'cls')
- class_sums: float32 [288, 2, 200, 128], P('dp', None, 'cls')
The draws below stay inside these ranges and needn't reach their ends.
All inputs are finite; a program needn't handle non-finite values.
Results may differ from the reference program's by a relative error of at most 0.0056.
Values may be sent and summed in bfloat16 or wider, within the bound.
A program may use at most 384 MiB of HBM per device.

```python
import math
import jax
import jax.numpy as jnp
from jax import lax

CYCLES = 128
ROTS = 36
ANG_STEP = 8
ANGLES = 288
SHIFT_SIDE = 5
CLASSES = 200
GROUPS = 16
PARTICLES = 256


def shared_integers(key):
    offsets = jax.random.randint(jax.random.fold_in(key, 11), (PARTICLES, 2), -8, 9).astype(jnp.int32)
    offsets = offsets.at[0, 0].set(8).at[0, 1].set(-8)
    groups = jax.random.randint(jax.random.fold_in(key, 12), (PARTICLES,), 0, GROUPS).astype(jnp.int32)
    particle_index = jnp.arange(PARTICLES, dtype=jnp.int32)
    groups = jnp.where(particle_index % 8 == 5, GROUPS - 1, groups).astype(jnp.int32)
    groups = groups.at[0].set(GROUPS - 1).at[1].set(0)
    rotation = jax.random.randint(jax.random.fold_in(key, 13), (CLASSES,), 0, ANG_STEP).astype(jnp.int32)
    rotation = rotation.at[0].set(ANG_STEP - 1).at[1].set(0)
    return (offsets, groups, rotation)


def shared_floats(key):
    spectra_all = jnp.clip(jax.random.normal(jax.random.fold_in(key, 21), (ANGLES, 2, CLASSES, CYCLES), jnp.float32), -6.0, 6.0) * 1.5
    amplitude = jnp.exp(jax.random.uniform(jax.random.fold_in(key, 23), (GROUPS, 1), jnp.float32, math.log(0.01), math.log(0.1)))
    amplitude = amplitude.at[GROUPS - 1, 0].set(0.1)
    ctf_rows = amplitude * jax.random.uniform(jax.random.fold_in(key, 22), (GROUPS, CYCLES), jnp.float32, -1.0, 1.0)
    return (spectra_all, ctf_rows)


def draw_references(key, part):
    return shared_floats(key)[0].astype(jnp.bfloat16)


def draw_ctf_table(key, part):
    return shared_floats(key)[1].astype(jnp.float32)


def draw_rot_offset(key, part):
    return shared_integers(key)[2]


def draw_prior_shift(key, part):
    return shared_integers(key)[0]


def draw_defocus_group(key, part):
    return shared_integers(key)[1]


def draw_particles(key, part):
    noise_field = jnp.clip(jax.random.normal(jax.random.fold_in(key, 31), (PARTICLES, 2, ANGLES, CYCLES), jnp.float32), -6.0, 6.0)
    return noise_field.astype(jnp.bfloat16)


def setup_inputs(seed: int = 0) -> dict:
    streams_of = jax.random.split(jax.random.key(seed), 7)
    return {
        "particles": draw_particles(jax.random.fold_in(streams_of[6], 71), 0),
        "references": draw_references(jax.random.fold_in(streams_of[6], 71), 0),
        "ctf_table": draw_ctf_table(jax.random.fold_in(streams_of[6], 71), 0),
        "rot_offset": draw_rot_offset(jax.random.fold_in(streams_of[6], 71), 0),
        "prior_shift": draw_prior_shift(jax.random.fold_in(streams_of[6], 71), 0),
        "defocus_group": draw_defocus_group(jax.random.fold_in(streams_of[6], 71), 0),
    }


two_pi = 2.0 * math.pi


def fourier_rows(angles):
    index_grid = jnp.arange(angles, dtype=jnp.int32)
    phase_index = (index_grid[:, None] * index_grid[None, :]) % angles
    radians = phase_index.astype(jnp.float32) * (two_pi / angles)
    cosine = jnp.cos(radians)
    sine_part = jnp.sin(radians)
    table_full = jnp.stack([jnp.stack([cosine, sine_part], 1), jnp.stack([-sine_part, cosine], 1)], 1)
    return table_full.reshape(2 * angles, 2 * angles).astype(jnp.bfloat16)


def rotation_tables(freq_rows, offsets, angles):
    rotation_steps = jnp.arange(ROTS, dtype=jnp.int32) * ANG_STEP
    angle_grid = rotation_steps[None, :] + offsets[:, None]
    phase_index = (freq_rows[:, None, None] * angle_grid[None, :, :]) % angles
    radians = phase_index.astype(jnp.float32) * (two_pi / angles)
    return jnp.cos(radians), jnp.sin(radians)


def reference(particles, references, ctf_table, rot_offset, prior_shift, defocus_group):
    angles = ANGLES
    cycles = CYCLES
    shifts = SHIFT_SIDE * SHIFT_SIDE
    top_score_value = lax.Precision.HIGHEST
    table_wide = fourier_rows(angles).astype(jnp.float32)
    spectra_all = references.astype(jnp.float32)
    power_sums = jnp.einsum('mxcr,gr->cg', spectra_all * spectra_all, ctf_table * ctf_table, precision=top_score_value)
    cos_all, sin_all = rotation_tables(jnp.arange(angles, dtype=jnp.int32), rot_offset, angles)
    theta_grid = jnp.arange(angles, dtype=jnp.int32).astype(jnp.float32) * (two_pi / angles)
    radius = (jnp.arange(cycles, dtype=jnp.int32) + 1).astype(jnp.float32) / (2.0 * cycles)
    shift_index = jnp.arange(shifts, dtype=jnp.int32)
    along_x = shift_index // SHIFT_SIDE - SHIFT_SIDE // 2
    along_y = shift_index % SHIFT_SIDE - SHIFT_SIDE // 2

    def one_particle(summed, inputs):
        image, offset, group = inputs
        shift_x = (offset[0] + along_x).astype(jnp.float32)
        shift_y = (offset[1] + along_y).astype(jnp.float32)
        argument = two_pi * radius[None, None, :] * (shift_x[None, :, None] * jnp.cos(theta_grid)[:, None, None]
                                                      + shift_y[None, :, None] * jnp.sin(theta_grid)[:, None, None])
        cosine = jnp.cos(argument)
        sine_part = jnp.sin(argument)
        real_part = image[0].astype(jnp.float32)[:, None, :]
        imag_part = image[1].astype(jnp.float32)[:, None, :]
        shifted = jnp.stack([real_part * cosine + imag_part * sine_part,
                             imag_part * cosine - real_part * sine_part]).astype(jnp.bfloat16)
        shifted = lax.optimization_barrier(shifted).astype(jnp.float32)
        spectrum = jnp.dot(table_wide, shifted.reshape(2 * angles, shifts * cycles), precision=top_score_value)
        spectrum = spectrum.reshape(angles, 2, shifts, cycles)
        ctf_row = ctf_table[group]
        weighted = (spectrum * ctf_row[None, None, None, :]).astype(jnp.bfloat16)
        weighted = lax.optimization_barrier(weighted).astype(jnp.float32)
        product = jnp.einsum('mxsr,mycr->mxsyc', weighted, spectra_all, precision=top_score_value)
        real_correlation = product[:, 0, :, 0] + product[:, 1, :, 1]
        imag_correlation = product[:, 1, :, 0] - product[:, 0, :, 1]
        cross_sums = (jnp.einsum('msc,mck->sck', real_correlation, cos_all, precision=top_score_value)
                      - jnp.einsum('msc,mck->sck', imag_correlation, sin_all, precision=top_score_value))
        class_power = power_sums[:, group]
        scores = cross_sums / angles - 0.5 * class_power[None, :, None] / angles
        peak_score = jnp.max(scores)
        log_total = peak_score + jnp.log(jnp.sum(jnp.exp(scores - peak_score)))
        weights = jnp.exp(scores - log_total)
        posterior = jnp.sum(weights, axis=(0, 2))
        real_returned = jnp.einsum('sck,mck->msc', weights, cos_all, precision=top_score_value).astype(jnp.bfloat16)
        imag_returned = jnp.einsum('sck,mck->msc', weights, sin_all, precision=top_score_value).astype(jnp.bfloat16)
        real_returned = lax.optimization_barrier(real_returned).astype(jnp.float32)
        imag_returned = lax.optimization_barrier(imag_returned).astype(jnp.float32)
        weighted_real = weighted[:, 0]
        weighted_imaginary = weighted[:, 1]
        real_accumulated = (jnp.einsum('jlh,jlv->jhv', real_returned, weighted_real, precision=top_score_value)
                    - jnp.einsum('jlh,jlv->jhv', imag_returned, weighted_imaginary, precision=top_score_value))
        imag_accumulated = (jnp.einsum('jlh,jlv->jhv', real_returned, weighted_imaginary, precision=top_score_value)
                    + jnp.einsum('jlh,jlv->jhv', imag_returned, weighted_real, precision=top_score_value))
        summed = summed + jnp.stack([real_accumulated, imag_accumulated], 1)
        return summed, (log_total, posterior)

    start_sums = jnp.zeros((angles, 2, CLASSES, cycles), jnp.float32)
    summed, outputs = lax.scan(one_particle, start_sums, (particles, prior_shift, defocus_group))
    log_evidence, class_posterior = outputs
    return log_evidence, class_posterior, summed
```

```python
import functools
import heapq
import math

import jax
import jax.numpy as jnp
import numpy as np
from jax import lax
from jax.experimental import pallas as pl
from jax.experimental.pallas import tpu as pltpu
from jax.sharding import PartitionSpec as P

ROTS = 36
SIDE = 5
SHIFTS = SIDE * SIDE
ANGLES = 288
CYCLES = 128
HALF = ANGLES // 2
REACH = 10
FOLD = ROTS // 2 + 1
IPAD = 80
QROWS = 208
CPAD = 64
F32 = jnp.float32
BF16 = jnp.bfloat16
MESH = pl.DeviceIdType.MESH


def phase_tables():
    order = np.concatenate([np.arange(0, ANGLES, 2), np.arange(1, ANGLES, 2)])
    theta = 2.0 * np.pi * order / ANGLES
    radius = (np.arange(CYCLES) + 1) / (2.0 * CYCLES)
    count = np.arange(REACH + 1)
    out = []
    for wave in (np.cos(theta), np.sin(theta)):
        arg = 2.0 * np.pi * count[:, None, None] * wave[None, :, None] * radius[None, None, :]
        out.append(np.stack([np.cos(arg), np.sin(arg)], 1).astype(np.float32))
    return out


def dft_tables():
    row = np.arange(IPAD)
    out = []
    for start in (0, 1):
        t = np.arange(start, ANGLES, 2)
        ang = 2.0 * np.pi * ((row[:, None] * t[None, :]) % ANGLES) / ANGLES
        out.append(np.concatenate([np.cos(ang), np.sin(ang)], 0).astype(np.float32))
    return out


def rotation_coefs():
    k = np.arange(FOLD)
    ang = 2.0 * np.pi * ((k[:, None] * k[None, :]) % ROTS) / ROTS
    cos, sin = np.cos(ang), np.sin(ang)
    lanes = np.arange(128) < CPAD
    fwd = np.where(lanes, cos[:, :, None], -sin[:, :, None]) / ANGLES
    bwd = np.where(lanes, cos[:, :, None], sin[:, :, None])
    return fwd.astype(np.float32), bwd.astype(np.float32)


def transform_kernel(shift, part, ctf, tx, ty, te, to, out, z1, xs, fr, fi):
    u = pl.program_id(0)

    def row(j, carry):
        s = jnp.minimum(2 * u + j // 8, SHIFTS - 1)
        p = j % 8
        a = s // SIDE
        b = s % SIDE

        @pl.when((b == 0))
        def _():
            sx = shift[p, 0] + a - SIDE // 2
            n = jnp.abs(sx)
            sg = jnp.where(sx < 0, -1.0, 1.0).astype(F32)
            for c in range(0, ANGLES, 48):
                rows = pl.ds(c, 48)
                re = part[p, 0, rows, :].astype(F32)
                im = part[p, 1, rows, :].astype(F32)
                co = tx[n, 0, rows, :]
                si = tx[n, 1, rows, :] * sg
                z1[p, 0, rows, :] = re * co + im * si
                z1[p, 1, rows, :] = im * co - re * si

        sy = shift[p, 1] + b - SIDE // 2
        n = jnp.abs(sy)
        sg = jnp.where(sy < 0, -1.0, 1.0).astype(F32)
        for c in range(0, ANGLES, 48):
            rows = pl.ds(c, 48)
            re = z1[p, 0, rows, :]
            im = z1[p, 1, rows, :]
            co = ty[n, 0, rows, :]
            si = ty[n, 1, rows, :] * sg
            xs[rows, 0:128] = (re * co + im * si).astype(BF16)
            xs[rows, 128:256] = (im * co - re * si).astype(BF16)
        even = jnp.dot(te[...], xs[0:HALF, :], preferred_element_type=F32)
        odd = jnp.dot(to[...], xs[HALF:, :], preferred_element_type=F32)
        gain = ctf[pl.ds(p, 1), :]
        for c in range(0, IPAD, 16):
            ce = even[c : c + 16] * jnp.concatenate([gain, gain], 1)
            se = even[IPAD + c : IPAD + c + 16] * jnp.concatenate([gain, gain], 1)
            co = odd[c : c + 16] * jnp.concatenate([gain, gain], 1)
            so = odd[IPAD + c : IPAD + c + 16] * jnp.concatenate([gain, gain], 1)
            u1 = ce[:, :128] + se[:, 128:]
            u2 = ce[:, :128] - se[:, 128:]
            v1 = co[:, :128] + so[:, 128:]
            v2 = co[:, :128] - so[:, 128:]
            w1 = ce[:, 128:] - se[:, :128]
            w2 = ce[:, 128:] + se[:, :128]
            y1 = co[:, 128:] - so[:, :128]
            y2 = co[:, 128:] + so[:, :128]
            for blk, (re, im) in enumerate(
                ((u1 + v1, w1 + y1), (u1 - v1, w1 - y1), (u2 - v2, w2 - y2), (u2 + v2, w2 + y2))
            ):
                at = pl.ds((blk * IPAD + c) * 16 + j, 16, stride=16)
                fr[at, :] = re
                fi[at, :] = im
        return carry

    lax.fori_loop(0, 16, row, 0)

    def emit(i, blk, m):
        at = pl.ds(pl.multiple_of((blk * IPAD + i) * 16, 16), 16)
        out[m, :, 0:128] = fr[at, :].astype(BF16)
        out[m, :, 128:256] = fi[at, :].astype(BF16)

    def pack(i, carry):
        emit(i, 0, i)
        emit(i, 1, HALF + i)
        emit(i, 2, HALF - i)
        emit(i, 3, ANGLES - i)
        return carry

    emit(0, 0, 0)
    emit(0, 1, HALF)
    emit(HALF // 2, 0, HALF // 2)
    emit(HALF // 2, 1, HALF + HALF // 2)
    lax.fori_loop(1, HALF // 2, pack, 0, unroll=2)


def transform(shift, part, ctf):
    tx, ty = phase_tables()
    te, to = dft_tables()
    whole = pl.BlockSpec(memory_space=pltpu.VMEM)
    return pl.pallas_call(
        transform_kernel,
        grid=(QROWS // 16,),
        out_shape=jax.ShapeDtypeStruct((ANGLES, QROWS, 256), BF16),
        in_specs=[pl.BlockSpec(memory_space=pltpu.SMEM)] + [whole] * 6,
        out_specs=pl.BlockSpec((ANGLES, 16, 256), lambda u: (0, u, 0)),
        scratch_shapes=[
            pltpu.VMEM((8, 2, ANGLES, 128), F32),
            pltpu.VMEM((ANGLES, 256), BF16),
            pltpu.VMEM((4 * IPAD * 16, 128), F32),
            pltpu.VMEM((4 * IPAD * 16, 128), F32),
        ],
        compiler_params=pltpu.CompilerParams(vmem_limit_bytes=56 * 2**20),
        name="transform",
    )(shift, part, ctf, jnp.asarray(tx), jnp.asarray(ty), jnp.asarray(te, BF16), jnp.asarray(to, BF16))


def match_kernel(block, wt, refs, ctf, fwd, bwd, spec, peak, mass, post, acc, power):
    d = pl.program_id(0)

    @pl.when(d == 0)
    def _():
        acc[...] = jnp.zeros_like(acc)
        power[...] = jnp.zeros_like(power)

    for i in range(block):
        m = d * block + i
        r = m % ROTS
        up = r <= ROTS // 2
        g = jnp.where(up, r, ROTS - r)
        sg = jnp.where(up, 1.0, -1.0).astype(BF16)
        ar = refs[0, 0, i]
        ai = refs[0, 1, i]
        table = jnp.concatenate(
            [jnp.concatenate([ar, ai], 1), jnp.concatenate([-ai * sg, ar * sg], 1)], 0
        )
        acc[g] += lax.dot_general(
            wt[i], table, (((1,), (1,)), ((), ())), preferred_element_type=F32
        )
        fa = ar.astype(F32)
        fb = ai.astype(F32)
        power[...] += fa * fa + fb * fb

    @pl.when(d == pl.num_programs(0) - 1)
    def _():
        gain = ctf[...]
        half = lax.dot_general(
            gain * gain,
            power[...],
            (((1,), (1,)), ((), ())),
            precision=lax.Precision.HIGHEST,
            preferred_element_type=F32,
        ) * (0.5 / ANGLES)
        bias = jnp.concatenate([half, half], 1)
        lane = lax.broadcasted_iota(jnp.int32, (8, 128), 1)
        live = lane % CPAD < classes_of
        edge = lane < classes_of
        sign = jnp.where(lane < CPAD, 1.0, -1.0).astype(F32)
        low = -1e30

        def score(s, top):
            rows = pl.ds(pl.multiple_of(s * 8, 8), 8)
            parts = [acc[g, rows, :] for g in range(FOLD)]
            for k in range(FOLD):
                y = parts[0] * fwd[k, 0:1, :]
                for g in range(1, FOLD):
                    y = y + parts[g] * fwd[k, g : g + 1, :]
                y = y * sign + pltpu.roll(y, CPAD, 1) - bias
                y = jnp.where(edge if k in (0, FOLD - 1) else live, y, low)
                spec[k, rows, :] = y
                top = jnp.maximum(top, y)
            return top

        top = lax.fori_loop(0, SHIFTS, score, jnp.full((8, 128), low, F32))
        top = jnp.max(top, axis=1, keepdims=True)

        def weigh(s, total):
            rows = pl.ds(pl.multiple_of(s * 8, 8), 8)
            parts = []
            for k in range(FOLD):
                e = jnp.exp(spec[k, rows, :] - top)
                total = total + e
                parts.append(e * sign + pltpu.roll(e, CPAD, 1))
            for g in range(FOLD):
                y = parts[0] * bwd[g, 0:1, :]
                for k in range(1, FOLD):
                    y = y + parts[k] * bwd[g, k : k + 1, :]
                spec[g, rows, :] = y
            return total

        total = lax.fori_loop(0, SHIFTS, weigh, jnp.zeros((8, 128), F32))
        spec[:, SHIFTS * 8 :, :] = jnp.zeros((FOLD, QROWS - SHIFTS * 8, 128), F32)
        peak[...] = jnp.broadcast_to(top, (8, 128))
        mass[...] = jnp.broadcast_to(jnp.sum(total, axis=1, keepdims=True), (8, 128))
        post[...] = total + pltpu.roll(total, CPAD, 1)


classes_of = 50


def match(wt, refs, ctf):
    fwd, bwd = rotation_coefs()
    owners, _, block = refs.shape[:3]
    small = jax.ShapeDtypeStruct((8, 128), F32)
    whole = pl.BlockSpec(memory_space=pltpu.VMEM)
    return pl.pallas_call(
        functools.partial(match_kernel, block),
        grid=(owners,),
        out_shape=(jax.ShapeDtypeStruct((FOLD, QROWS, 128), F32), small, small, small),
        in_specs=[
            pl.BlockSpec((block, QROWS, 256), lambda d: (d, 0, 0)),
            pl.BlockSpec((1, 2, block, CPAD, 128), lambda d: (d, 0, 0, 0, 0)),
            whole,
            whole,
            whole,
        ],
        out_specs=(whole,) * 4,
        scratch_shapes=[pltpu.VMEM((FOLD, QROWS, 128), F32), pltpu.VMEM((CPAD, 128), F32)],
        compiler_params=pltpu.CompilerParams(vmem_limit_bytes=48 * 2**20),
        name="match",
    )(wt, refs, ctf, jnp.asarray(fwd), jnp.asarray(bwd))


def back_kernel(block, wt, spec, scale, out, tab):
    d = pl.program_id(0)

    @pl.when(d == 0)
    def _():
        for g in range(FOLD):
            rows = spec[g] * jnp.concatenate([scale[...]] * (QROWS // 8), 0)
            tab[g] = rows.T.astype(BF16)

    for i in range(block):
        m = d * block + i
        r = m % ROTS
        up = r <= ROTS // 2
        g = jnp.where(up, r, ROTS - r)
        sg = jnp.where(up, 1.0, -1.0).astype(F32)
        both = jnp.dot(tab[g], wt[i], preferred_element_type=F32)
        out[0, 0, i] = (both[:CPAD, :128] - sg * both[CPAD:, 128:]).astype(BF16)
        out[0, 1, i] = (both[:CPAD, 128:] + sg * both[CPAD:, :128]).astype(BF16)


def back(wt, spec, scale, owners):
    block = ANGLES // owners
    whole = pl.BlockSpec(memory_space=pltpu.VMEM)
    return pl.pallas_call(
        functools.partial(back_kernel, block),
        grid=(owners,),
        out_shape=jax.ShapeDtypeStruct((owners, 2, block, CPAD, 128), BF16),
        in_specs=[pl.BlockSpec((block, QROWS, 256), lambda d: (d, 0, 0)), whole, whole],
        out_specs=pl.BlockSpec((1, 2, block, CPAD, 128), lambda d: (d, 0, 0, 0, 0)),
        scratch_shapes=[pltpu.VMEM((FOLD, 128, QROWS), BF16)],
        compiler_params=pltpu.CompilerParams(vmem_limit_bytes=48 * 2**20),
        name="back",
    )(wt, spec, scale)


def twist_tables(freq, rot_offset):
    idx = (freq[:, None] * rot_offset[None, :]) % ANGLES
    rad = idx.astype(F32) * (2.0 * math.pi / ANGLES)
    return jnp.cos(rad)[:, :, None], jnp.sin(rad)[:, :, None]


def twist_refs(references, cos, sin):
    re = references[:, 0].astype(F32)
    im = references[:, 1].astype(F32)
    both = jnp.stack([re * cos + im * sin, im * cos - re * sin], 0)
    return jnp.pad(both, ((0, 0), (0, 0), (0, CPAD - both.shape[2]), (0, 0))).astype(BF16)


def untwist(sums, cos, sin, classes):
    re = sums[0, :, :classes].astype(F32)
    im = sums[1, :, :classes].astype(F32)
    return jnp.stack([re * cos - im * sin, re * sin + im * cos], 1)


def order_angles(particles):
    return jnp.concatenate([particles[:, :, 0::2], particles[:, :, 1::2]], 2)


def group_rows(defocus_group, ctf_table):
    hit = defocus_group[:, None] == jnp.arange(ctf_table.shape[0], dtype=jnp.int32)[None, :]
    return jnp.sum(jnp.where(hit[:, :, None], ctf_table[None], 0.0), 1)
SIZES = (4, 2, 4)
SUB = (5, 4)
LATE = 0.5


def place():
    dp = lax.axis_index("dp")
    return dp % 4, (dp // 4) % 2, dp // 8, lax.axis_index("cls")


def peer(me, rel):
    x, y, z, cls = me
    return ((((z + rel[2]) % 4) * 2 + (y + rel[1]) % 2) * 4 + (x + rel[0]) % 4, cls)


def slot(me, rel):
    return peer(me, rel)[0]


def toward(axis, sign):
    move = [0, 0, 0]
    move[axis] = sign
    return tuple(move)


def greet(me):
    barrier = pltpu.get_barrier_semaphore()
    moves = [toward(0, 1), toward(0, -1), toward(1, 1), toward(2, 1), toward(2, -1)]
    for move in moves:
        pl.semaphore_signal(barrier, inc=1, device_id=peer(me, move), device_id_type=MESH)
    pl.semaphore_wait(barrier, len(moves))


def axes_of(half):
    return (0, 1, 2) if half == 0 else (2, 1, 0)


def span(sub):
    return pl.ds(0, sum(SUB)) if sub is None else pl.ds(0 if sub == 0 else SUB[0], SUB[sub])


class Links:
    def __init__(self):
        self.free, self.heap, self.count = {}, [], 0

    def send(self, t, axis, sign, size, key):
        start = max(t, self.free.get((axis, sign), 0.0))
        self.free[(axis, sign)] = start + size
        self.push(start + size + LATE, key)

    def push(self, t, key):
        self.count += 1
        heapq.heappush(self.heap, (t, self.count, key))

    def pop(self):
        t, _, key = heapq.heappop(self.heap)
        return t, key


def gather_plan():
    links, plan, got = Links(), [], {}
    for half in (0, 1):
        links.push(0.0, (half, (0, 0, 0), None))
    while links.heap:
        t, key = links.pop()
        half, rel, sub = key
        order = axes_of(half)
        sends = []

        def go(axis, sign, sub):
            seen = list(rel)
            seen[axis] = (seen[axis] - sign) % SIZES[axis]
            there = (half, tuple(seen), sub)
            sends.append((half, rel, sub, axis, sign, there))
            links.send(t, axis, sign, 1.0 if sub is None else SUB[sub] / sum(SUB), there)

        got[half, rel] = got.get((half, rel), 0) + 1
        if sub is None or got[half, rel] == 2:
            last = max([i for i in range(3) if rel[order[i]]], default=-1)
            for i in range(2, last, -1):
                if order[i] == 1:
                    go(1, 1, None)
                else:
                    go(order[i], 1, None)
                    go(order[i], -1, None)
            if last >= 0 and order[last] != 1:
                if rel[order[last]] == 3:
                    go(order[last], 1, 0)
                elif rel[order[last]] == 1:
                    go(order[last], -1, 1)
        plan.append((t, None if rel == (0, 0, 0) else key, sends))
    return plan


def gather_keys():
    plan = gather_plan()
    recv = {step[1]: i for i, step in enumerate(s for s in plan if s[1] is not None)}
    return plan, recv


class Gather:
    def __init__(self, me, own, store, send_sem, recv_sem):
        self.me, self.own, self.store = me, own, store
        self.send_sem, self.recv_sem = send_sem, recv_sem
        self.plan, self.recv = gather_keys()
        self.sent = []

    def copy(self, index, half, rel, sub, axis, sign, there):
        where = span(sub)
        here = self.own.at[half, where] if rel == (0, 0, 0) else self.store.at[slot(self.me, rel), half, where]
        return pltpu.make_async_remote_copy(
            src_ref=here,
            dst_ref=self.store.at[slot(self.me, rel), half, where],
            send_sem=self.send_sem.at[index],
            recv_sem=self.recv_sem.at[self.recv[there]],
            device_id=peer(self.me, toward(axis, sign)),
            device_id_type=MESH,
        )

    def arrived(self, key):
        half, rel, sub = key
        here = self.store.at[slot(self.me, rel), half, span(sub)]
        pltpu.make_async_remote_copy(
            src_ref=here,
            dst_ref=here,
            send_sem=self.send_sem.at[0],
            recv_sem=self.recv_sem.at[self.recv[key]],
            device_id=peer(self.me, (1, 0, 0)),
            device_id_type=MESH,
        ).wait_recv()

    def step(self, item):
        _, key, sends = item
        if key is not None:
            self.arrived(key)
        for send in sends:
            copy = self.copy(len(self.sent), *send)
            copy.start()
            self.sent.append(copy)

    def finish(self):
        for copy in self.sent:
            copy.wait_send()


def gather_kernel(own, store, send_sem, recv_sem, own_sem):
    me = place()
    greet(me)
    keep = pltpu.make_async_copy(own, store.at[slot(me, (0, 0, 0))], own_sem)
    keep.start()
    work = Gather(me, own, store, send_sem, recv_sem)
    for item in work.plan:
        work.step(item)
    work.finish()
    keep.wait()


def gather(own):
    plan, recv = gather_keys()
    owners = SIZES[0] * SIZES[1] * SIZES[2]
    return pl.pallas_call(
        gather_kernel,
        out_shape=jax.ShapeDtypeStruct((owners,) + own.shape, own.dtype),
        in_specs=[pl.BlockSpec(memory_space=pltpu.VMEM)],
        out_specs=pl.BlockSpec(memory_space=pl.ANY),
        scratch_shapes=[
            pltpu.SemaphoreType.DMA((sum(len(s[2]) for s in plan),)),
            pltpu.SemaphoreType.DMA((len(recv),)),
            pltpu.SemaphoreType.DMA,
        ],
        compiler_params=pltpu.CompilerParams(
            collective_id=1, has_side_effects=True, vmem_limit_bytes=16 * 2**20
        ),
        name="gather",
    )(own)


COMBOS = [(ry, c) for ry in (1, 0) for c in (2, 1, 3, 0)]


def scatter_plan(ready=None):
    links, steps, got = Links(), [], set()
    done = set()

    def send(t, half, stage, combo, kind):
        order = axes_of(half)[::-1]
        axis = order[stage]
        sign = 1 if kind in ("a0", "l0", "l1", "y") else -1
        size = 1.0 if kind == "y" else SUB[int(kind[1])] / sum(SUB)
        msg = (half, stage, combo, kind)
        steps.append(("send", msg))
        links.send(t, axis, sign, size, msg)

    def first(t, half, stage, combo, k):
        if k == 2:
            send(t, half, stage, combo, "a0")
            send(t, half, stage, combo, "a1")
        elif k == 1:
            send(t, half, stage, combo, "l1")
        elif k == 3:
            send(t, half, stage, combo, "r0")

    def second(t, half, c):
        if (half, 0, (0, c), "s") in done and (half, 1, c, "y") in got:
            steps.append(("pair", (half, c)))
            done.add((half, 2, c))
            first(t, half, 2, None, c)
            if c == 1:
                relay(t, half, 2, None, "a0")
            if c == 3:
                relay(t, half, 2, None, "a1")
            if c == 0:
                total(t, half, 2, None)

    def have(half, stage, k):
        return stage == 0 or (half, 2, k) in done

    def relay(t, half, stage, combo, kind):
        k = 1 if kind == "a0" else 3
        if (half, stage, combo, kind) in got and have(half, stage, k):
            steps.append(("relay", (half, stage, combo, kind)))
            send(t, half, stage, combo, "l0" if kind == "a0" else "r1")

    def total(t, half, stage, combo):
        if all((half, stage, combo, kind) in got for kind in ("l0", "l1", "r0", "r1")) and have(
            half, stage, 0
        ):
            steps.append(("total", (half, stage, combo)))
            if stage == 0:
                done.add((half, 0, combo, "s"))
                if combo[0] == 1:
                    send(t, half, 1, combo[1], "y")
                else:
                    second(t, half, combo[1])

    for k in (2, 1, 3):
        for combo in COMBOS:
            for half in (0, 1):
                first(0.0, half, 0, combo, k)
    while links.heap:
        t, msg = links.pop()
        half, stage, combo, kind = msg
        steps.append(("wait", msg))
        got.add(msg)
        if kind == "y":
            second(t, half, combo)
        elif kind in ("a0", "a1"):
            relay(t, half, stage, combo, kind)
        else:
            total(t, half, stage, combo)
    return steps


def scatter_keys():
    steps = scatter_plan()
    return steps, {s[1]: i for i, s in enumerate(s for s in steps if s[0] == "send")}


class Scatter:
    def __init__(self, me, own, three, pair, out, send_sem, recv_sem):
        self.me, self.own, self.three, self.pair, self.out = me, own, three, pair, out
        self.send_sem, self.recv_sem = send_sem, recv_sem
        self.steps, self.index = scatter_keys()
        self.sent = []

    def group(self, stage, combo):
        return 8 if stage == 2 else COMBOS.index(combo)

    def mine(self, half, stage, combo, k):
        if stage == 2:
            return self.pair.at[half, k]
        order = axes_of(half)[::-1]
        rel = [0, 0, 0]
        rel[order[0]] = k
        rel[1] = combo[0]
        rel[order[2]] = combo[1]
        return self.own.at[slot(self.me, rel), half]

    def box(self, msg):
        half, stage, combo, kind = msg
        if kind == "y":
            return self.pair.at[half, combo]
        which = {"a": 0, "l": 1, "r": 2}[kind[0]]
        return self.three.at[half, self.group(stage, combo), which, span(int(kind[1]))]

    def source(self, msg):
        half, stage, combo, kind = msg
        if kind == "y":
            return self.three.at[half, self.group(0, (1, combo)), 1]
        where = span(int(kind[1]))
        if kind in ("a0", "a1"):
            return self.mine(half, stage, combo, 2).at[where]
        if kind == "l1":
            return self.mine(half, stage, combo, 1).at[where]
        if kind == "r0":
            return self.mine(half, stage, combo, 3).at[where]
        return self.three.at[half, self.group(stage, combo), 0, where]

    def copy(self, msg, src=None):
        half, stage, combo, kind = msg
        axis = axes_of(half)[::-1][stage]
        sign = 1 if kind in ("a0", "l0", "l1", "y") else -1
        i = self.index[msg]
        box = self.box(msg)
        return pltpu.make_async_remote_copy(
            src_ref=box if src is None else src,
            dst_ref=box,
            send_sem=self.send_sem.at[i],
            recv_sem=self.recv_sem.at[i],
            device_id=peer(self.me, toward(axis, sign)),
            device_id_type=MESH,
        )

    def add(self, dst, terms, count):
        def one(i, carry):
            value = terms[0][i].astype(F32)
            for term in terms[1:]:
                value = value + term[i].astype(F32)
            dst[i] = value.astype(dst.dtype)
            return carry

        lax.fori_loop(0, count, one, 0)

    def step(self, item):
        what, key = item
        if what == "send":
            copy = self.copy(key, self.source(key))
            copy.start()
            self.sent.append(copy)
        elif what == "wait":
            self.copy(key).wait_recv()
        elif what == "relay":
            half, stage, combo, kind = key
            box = self.box(key)
            mine = self.mine(half, stage, combo, 1 if kind == "a0" else 3).at[span(int(kind[1]))]
            self.add(box, (mine, box), SUB[int(kind[1])])
        elif what == "pair":
            half, c = key
            box = self.pair.at[half, c]
            self.add(box, (self.three.at[half, self.group(0, (0, c)), 1], box), sum(SUB))
        else:
            half, stage, combo = key
            left = self.three.at[half, self.group(stage, combo), 1]
            right = self.three.at[half, self.group(stage, combo), 2]
            mine = self.mine(half, stage, combo, 0)
            dst = self.out.at[half] if stage == 2 else left
            self.add(dst, (mine, left, right), sum(SUB))

    def finish(self):
        for copy in self.sent:
            copy.wait_send()


def scatter_kernel(own, out, three, pair, send_sem, recv_sem):
    me = place()
    greet(me)
    work = Scatter(me, own, three, pair, out, send_sem, recv_sem)
    for item in work.steps:
        work.step(item)
    work.finish()


def scatter(own):
    steps, index = scatter_keys()
    block = own.shape[2:]
    return pl.pallas_call(
        scatter_kernel,
        out_shape=jax.ShapeDtypeStruct((2,) + block, F32),
        in_specs=[pl.BlockSpec(memory_space=pltpu.VMEM)],
        out_specs=pl.BlockSpec(memory_space=pltpu.VMEM),
        scratch_shapes=[
            pltpu.VMEM((2, 9, 3) + block, BF16),
            pltpu.VMEM((2, 4) + block, BF16),
            pltpu.SemaphoreType.DMA((len(index),)),
            pltpu.SemaphoreType.DMA((len(index),)),
        ],
        compiler_params=pltpu.CompilerParams(
            collective_id=2, has_side_effects=True, vmem_limit_bytes=48 * 2**20
        ),
        name="scatter",
    )(own)


def local(particles, references, ctf_table, rot_offset, prior_shift, defocus_group):
    owners = lax.axis_size("dp")
    block, _, classes = references.shape[:3]
    freq = lax.axis_index("dp") * block + jnp.arange(block, dtype=jnp.int32)
    cos, sin = twist_tables(freq, rot_offset)
    refs = gather(twist_refs(references, cos, sin))
    ctf = group_rows(defocus_group, ctf_table)
    wt = transform(prior_shift, order_angles(particles), ctf)
    spec, peak, mass, post = match(wt, refs, ctf)
    top = lax.pmax(peak[:, 0], "cls")
    log_evidence = top + jnp.log(lax.psum(mass[:, 0] * jnp.exp(peak[:, 0] - top), "cls"))
    scale = jnp.exp(peak - log_evidence[:, None])
    sums = scatter(back(wt, spec, scale, owners))
    return (
        log_evidence,
        post[:, :classes] * scale[:, :classes],
        untwist(sums, cos, sin, classes),
    )


def solution(mesh):
    placed = (
        P("dp", None, None, None),
        P("dp", None, "cls", None),
        P(),
        P("cls"),
        P("dp", None),
        P("dp"),
    )
    return jax.shard_map(
        local,
        mesh=mesh,
        in_specs=placed,
        out_specs=(P("dp"), P("dp", "cls"), P("dp", None, "cls", None)),
        check_vma=False,
    )
```

```python
import functools
import heapq
import math

import jax
import jax.numpy as jnp
import numpy as np
from jax import lax
from jax.experimental import pallas as pl
from jax.experimental.pallas import tpu as pltpu
from jax.sharding import PartitionSpec as P

ROTS = 36
SIDE = 5
SHIFTS = SIDE * SIDE
ANGLES = 288
CYCLES = 128
HALF = ANGLES // 2
REACH = 10
FOLD = ROTS // 2 + 1
IPAD = 80
QROWS = 208
CPAD = 64
F32 = jnp.float32
BF16 = jnp.bfloat16
MESH = pl.DeviceIdType.MESH


def phase_tables():
    order = np.concatenate([np.arange(0, ANGLES, 2), np.arange(1, ANGLES, 2)])
    theta = 2.0 * np.pi * order / ANGLES
    radius = (np.arange(CYCLES) + 1) / (2.0 * CYCLES)
    count = np.arange(REACH + 1)
    out = []
    for wave in (np.cos(theta), np.sin(theta)):
        arg = 2.0 * np.pi * count[:, None, None] * wave[None, :, None] * radius[None, None, :]
        out.append(np.stack([np.cos(arg), np.sin(arg)], 1).astype(np.float32))
    return out


def dft_tables():
    row = np.arange(IPAD)
    out = []
    for start in (0, 1):
        t = np.arange(start, ANGLES, 2)
        ang = 2.0 * np.pi * ((row[:, None] * t[None, :]) % ANGLES) / ANGLES
        out.append(np.concatenate([np.cos(ang), np.sin(ang)], 0).astype(np.float32))
    return out


def rotation_coefs():
    k = np.arange(FOLD)
    ang = 2.0 * np.pi * ((k[:, None] * k[None, :]) % ROTS) / ROTS
    cos, sin = np.cos(ang), np.sin(ang)
    lanes = np.arange(128) < CPAD
    fwd = np.where(lanes, cos[:, :, None], -sin[:, :, None]) / ANGLES
    bwd = np.where(lanes, cos[:, :, None], sin[:, :, None])
    return fwd.astype(np.float32), bwd.astype(np.float32)


SIZES = (4, 2, 4)
SUB = (5, 4)
LATE = 0.5


def place():
    dp = lax.axis_index("dp")
    return dp % 4, (dp // 4) % 2, dp // 8, lax.axis_index("cls")


def peer(me, rel):
    x, y, z, cls = me
    return ((((z + rel[2]) % 4) * 2 + (y + rel[1]) % 2) * 4 + (x + rel[0]) % 4, cls)


def slot(me, rel):
    return peer(me, rel)[0]


def toward(axis, sign):
    move = [0, 0, 0]
    move[axis] = sign
    return tuple(move)


def greet(me):
    barrier = pltpu.get_barrier_semaphore()
    moves = [toward(0, 1), toward(0, -1), toward(1, 1), toward(2, 1), toward(2, -1)]
    for move in moves:
        pl.semaphore_signal(barrier, inc=1, device_id=peer(me, move), device_id_type=MESH)
    pl.semaphore_wait(barrier, len(moves))


def axes_of(half):
    return (0, 1, 2) if half == 0 else (2, 1, 0)


def span(sub):
    return pl.ds(0, sum(SUB)) if sub is None else pl.ds(0 if sub == 0 else SUB[0], SUB[sub])


class Links:
    def __init__(self):
        self.free, self.heap, self.count = {}, [], 0

    def send(self, t, axis, sign, size, key):
        start = max(t, self.free.get((axis, sign), 0.0))
        self.free[(axis, sign)] = start + size
        self.push(start + size + LATE, key)

    def push(self, t, key):
        self.count += 1
        heapq.heappush(self.heap, (t, self.count, key))

    def pop(self):
        t, _, key = heapq.heappop(self.heap)
        return t, key


def gather_plan():
    links, plan, got = Links(), [], {}
    for half in (0, 1):
        links.push(0.0, (half, (0, 0, 0), None))
    while links.heap:
        t, key = links.pop()
        half, rel, sub = key
        order = axes_of(half)
        sends = []

        def go(axis, sign, sub):
            seen = list(rel)
            seen[axis] = (seen[axis] - sign) % SIZES[axis]
            there = (half, tuple(seen), sub)
            sends.append((half, rel, sub, axis, sign, there))
            links.send(t, axis, sign, 1.0 if sub is None else SUB[sub] / sum(SUB), there)

        got[half, rel] = got.get((half, rel), 0) + 1
        if sub is None or got[half, rel] == 2:
            last = max([i for i in range(3) if rel[order[i]]], default=-1)
            for i in range(2, last, -1):
                if order[i] == 1:
                    go(1, 1, None)
                else:
                    go(order[i], 1, None)
                    go(order[i], -1, None)
            if last >= 0 and order[last] != 1:
                if rel[order[last]] == 3:
                    go(order[last], 1, 0)
                elif rel[order[last]] == 1:
                    go(order[last], -1, 1)
        plan.append((t, None if rel == (0, 0, 0) else key, sends))
    return plan


def gather_keys():
    plan = gather_plan()
    recv = {step[1]: i for i, step in enumerate(s for s in plan if s[1] is not None)}
    return plan, recv


class Gather:
    def __init__(self, me, own, store, send_sem, recv_sem):
        self.me, self.own, self.store = me, own, store
        self.send_sem, self.recv_sem = send_sem, recv_sem
        self.plan, self.recv = gather_keys()
        self.sent = []

    def copy(self, index, half, rel, sub, axis, sign, there):
        where = span(sub)
        here = self.own.at[half, where] if rel == (0, 0, 0) else self.store.at[slot(self.me, rel), half, where]
        return pltpu.make_async_remote_copy(
            src_ref=here,
            dst_ref=self.store.at[slot(self.me, rel), half, where],
            send_sem=self.send_sem.at[index],
            recv_sem=self.recv_sem.at[self.recv[there]],
            device_id=peer(self.me, toward(axis, sign)),
            device_id_type=MESH,
        )

    def arrived(self, key):
        half, rel, sub = key
        here = self.store.at[slot(self.me, rel), half, span(sub)]
        pltpu.make_async_remote_copy(
            src_ref=here,
            dst_ref=here,
            send_sem=self.send_sem.at[0],
            recv_sem=self.recv_sem.at[self.recv[key]],
            device_id=peer(self.me, (1, 0, 0)),
            device_id_type=MESH,
        ).wait_recv()

    def step(self, item):
        _, key, sends = item
        if key is not None:
            self.arrived(key)
        for send in sends:
            self.copy(len(self.sent), *send).start()
            self.sent.append(send)

    def finish(self):
        for index, send in enumerate(self.sent):
            self.copy(index, *send).wait_send()


GROUP = 8
STEPS = 26
PITCH = 4 * IPAD + 1
UNIT_STEPS = 2.06


def transform_kernel(shift, part, ctf, tx, ty, te, to, own, out, store, z1, xs, fr, fi, send_sem, recv_sem, own_sem):
    u = pl.program_id(0)
    me = place()
    work = Gather(me, own, store, send_sem, recv_sem)
    keep = pltpu.make_async_copy(own, store.at[slot(me, (0, 0, 0))], own_sem)
    due = {}
    for item in work.plan:
        at = 0 if item[1] is None else min(STEPS - 1, math.ceil(item[0] * UNIT_STEPS))
        due.setdefault(at, []).append(item)

    @pl.when(u == 0)
    def _():
        greet(me)
        keep.start()

    for at in sorted(due):
        if at < STEPS - 1:

            @pl.when(u == at)
            def _(at=at):
                for item in due[at]:
                    work.step(item)

    s = jnp.minimum(u, SHIFTS - 1)
    a = s // SIDE
    b = s % SIDE

    @pl.when((b == 0) & (u < SHIFTS))
    def _():
        def ramp(p, carry):
            sx = shift[p, 0] + a - SIDE // 2
            n = jnp.abs(sx)
            sg = jnp.where(sx < 0, -1.0, 1.0).astype(F32)
            for c in range(0, ANGLES, 48):
                rows = pl.ds(c, 48)
                re = part[p, 0, rows, :].astype(F32)
                im = part[p, 1, rows, :].astype(F32)
                co = tx[n, 0, rows, :]
                si = tx[n, 1, rows, :] * sg
                z1[p, 0, rows, :] = re * co + im * si
                z1[p, 1, rows, :] = im * co - re * si
            return carry

        lax.fori_loop(0, GROUP, ramp, 0)

    @pl.when(u < SHIFTS)
    def _():
        for p in range(GROUP):
            sy = shift[p, 1] + b - SIDE // 2
            n = jnp.abs(sy)
            sg = jnp.where(sy < 0, -1.0, 1.0).astype(F32)
            for c in range(0, ANGLES, 16):
                rows = pl.ds(c, 16)
                re = z1[p, 0, rows, :]
                im = z1[p, 1, rows, :]
                co = ty[n, 0, rows, :]
                si = ty[n, 1, rows, :] * sg
                xs[rows, 256 * p : 256 * p + 128] = (re * co + im * si).astype(BF16)
                xs[rows, 256 * p + 128 : 256 * p + 256] = (im * co - re * si).astype(BF16)
        even = jnp.dot(te[...], xs[0:HALF, :], preferred_element_type=F32)
        odd = jnp.dot(to[...], xs[HALF:, :], preferred_element_type=F32)
        for p in range(GROUP):
            j = (u % 2) * GROUP + p
            gain = ctf[p : p + 1, :]
            lo, hi = slice(256 * p, 256 * p + 128), slice(256 * p + 128, 256 * p + 256)
            for c in range(0, IPAD, 8):
                cos, sin = slice(c, c + 8), slice(IPAD + c, IPAD + c + 8)
                u1 = (even[cos, lo] + even[sin, hi]) * gain
                u2 = (even[cos, lo] - even[sin, hi]) * gain
                w1 = (even[cos, hi] - even[sin, lo]) * gain
                w2 = (even[cos, hi] + even[sin, lo]) * gain
                v1 = (odd[cos, lo] + odd[sin, hi]) * gain
                v2 = (odd[cos, lo] - odd[sin, hi]) * gain
                y1 = (odd[cos, hi] - odd[sin, lo]) * gain
                y2 = (odd[cos, hi] + odd[sin, lo]) * gain
                for blk, (re, im) in enumerate(
                    ((u1 + v1, w1 + y1), (u1 - v1, w1 - y1), (u2 - v2, w2 - y2), (u2 + v2, w2 + y2))
                ):
                    rows = pl.ds(j * PITCH + blk * IPAD + c, 8)
                    fr[rows, :] = re
                    fi[rows, :] = im

    def emit(i, blk, m):
        rows = pl.ds(blk * IPAD + i, 2 * GROUP, stride=PITCH)
        out[m, :, 0:128] = fr[rows, :].astype(BF16)
        out[m, :, 128:256] = fi[rows, :].astype(BF16)

    @pl.when(u % 2 == 1)
    def _():
        def pack(i, carry):
            emit(i, 0, i)
            emit(i, 1, HALF + i)
            emit(i, 2, HALF - i)
            emit(i, 3, ANGLES - i)
            return carry

        emit(0, 0, 0)
        emit(0, 1, HALF)
        emit(HALF // 2, 0, HALF // 2)
        emit(HALF // 2, 1, HALF + HALF // 2)
        lax.fori_loop(1, HALF // 2, pack, 0, unroll=8)

    @pl.when(u == STEPS - 1)
    def _():
        for item in due.get(STEPS - 1, []):
            work.step(item)
        keep.wait()
        work.finish()


def transform(shift, part, ctf, own):
    tx, ty = phase_tables()
    te, to = dft_tables()
    plan, recv = gather_keys()
    whole = pl.BlockSpec(memory_space=pltpu.VMEM)
    owners = SIZES[0] * SIZES[1] * SIZES[2]
    return pl.pallas_call(
        transform_kernel,
        grid=(STEPS,),
        out_shape=(
            jax.ShapeDtypeStruct((ANGLES, QROWS, 256), BF16),
            jax.ShapeDtypeStruct((owners,) + own.shape, own.dtype),
        ),
        in_specs=[pl.BlockSpec(memory_space=pltpu.SMEM)] + [whole] * 7,
        out_specs=(
            pl.BlockSpec((ANGLES, 2 * GROUP, 256), lambda u: (0, u // 2, 0)),
            pl.BlockSpec(memory_space=pl.ANY),
        ),
        scratch_shapes=[
            pltpu.VMEM((GROUP, 2, ANGLES, 128), F32),
            pltpu.VMEM((ANGLES, 256 * GROUP), BF16),
            pltpu.VMEM((2 * GROUP * PITCH + 8, 128), F32),
            pltpu.VMEM((2 * GROUP * PITCH + 8, 128), F32),
            pltpu.SemaphoreType.DMA((sum(len(s[2]) for s in plan),)),
            pltpu.SemaphoreType.DMA((len(recv),)),
            pltpu.SemaphoreType.DMA,
        ],
        compiler_params=pltpu.CompilerParams(
            collective_id=1, has_side_effects=True, vmem_limit_bytes=56 * 2**20
        ),
        name="transform",
    )(shift, part, ctf, jnp.asarray(tx), jnp.asarray(ty), jnp.asarray(te, BF16), jnp.asarray(to, BF16), own)


H = FOLD // 2

def fold_of(r):
    return (r, 1) if r <= ROTS // 2 else (ROTS - r, -1)

def swap(t):
    return jnp.concatenate([t[:, CPAD:], t[:, :CPAD]], 1)

def half_sums(parts, tab, k):
    even = parts[0] * tab[k, 0:1, :]
    for g in range(2, FOLD, 2):
        even = even + parts[g] * tab[k, g : g + 1, :]
    odd = parts[1] * tab[k, 1:2, :]
    for g in range(3, FOLD, 2):
        odd = odd + parts[g] * tab[k, g : g + 1, :]
    return even, odd

def match_kernel(classes, wt, refs, ctf, fwd, bwd, spec, peak, mass, post, acc, power):
    d = pl.program_id(0)
    first = d == 0
    lanes = lax.broadcasted_iota(jnp.int32, (128, 128), 1)
    minus_high = jnp.where(lanes < CPAD, 1.0, -1.0).astype(BF16)

    def image(r):
        return jnp.concatenate([refs[r // 9, 0, r % 9], refs[r // 9, 1, r % 9]], 0)

    def product(r):
        t = image(r)
        if fold_of(r)[1] > 0:
            table = jnp.concatenate([t * minus_high, swap(t)], 0)
        else:
            table = jnp.concatenate([t, swap(t) * minus_high], 0)
        return jnp.dot(wt[r], table, preferred_element_type=F32)

    @pl.when(first)
    def _():
        acc[...] = jnp.zeros_like(acc)
        power[...] = jnp.zeros_like(power)

    for g in range(FOLD):
        y = product(g)
        if 0 < g < FOLD - 1:
            y = y + product(ROTS - g)
        acc[g] += y
    pw = power[...]
    for r in range(ROTS):
        tf = image(r).astype(F32)
        pw = pw + tf * tf
    power[...] = pw

    @pl.when(d == pl.num_programs(0) - 1)
    def _():
        gain = ctf[...]
        half = jnp.dot(
            gain * gain, power[...], precision=lax.Precision.HIGHEST, preferred_element_type=F32
        ) * (0.5 / ANGLES)
        bias = half + pltpu.roll(half, CPAD, 1)
        lane = lax.broadcasted_iota(jnp.int32, (8, 128), 1)
        live = lane % CPAD < classes
        edge = lane < classes
        sign = jnp.where(lane < CPAD, 1.0, -1.0).astype(F32)
        low = -1e30

        def score(s, top):
            rows = pl.ds(pl.multiple_of(s * 8, 8), 8)
            parts = [acc[g, rows, :] for g in range(FOLD)]
            for k in range(H + 1):
                even, odd = half_sums(parts, fwd, k)
                y, w = even + odd, even - odd
                both = [(k, y * sign + pltpu.roll(y, CPAD, 1))]
                if k < H:
                    both.append((FOLD - 1 - k, w + pltpu.roll(w * sign, CPAD, 1)))
                for at, z in both:
                    z = z - bias
                    z = jnp.where(edge if at in (0, FOLD - 1) else live, z, low)
                    spec[at, rows, :] = z
                    top = jnp.maximum(top, z)
            return top

        top = lax.fori_loop(0, SHIFTS, score, jnp.full((8, 128), low, F32))
        top = jnp.max(top, axis=1, keepdims=True)

        def weigh(s, total):
            rows = pl.ds(pl.multiple_of(s * 8, 8), 8)
            parts = []
            for k in range(FOLD):
                e = jnp.exp(spec[k, rows, :] - top)
                total = total + e
                parts.append(e * sign + pltpu.roll(e, CPAD, 1))
            for g in range(H + 1):
                even, odd = half_sums(parts, bwd, g)
                spec[g, rows, :] = even + odd
                if g < H:
                    spec[FOLD - 1 - g, rows, :] = (even - odd) * sign
            return total

        total = lax.fori_loop(0, SHIFTS, weigh, jnp.zeros((8, 128), F32))
        spec[:, SHIFTS * 8 :, :] = jnp.zeros((FOLD, QROWS - SHIFTS * 8, 128), F32)
        peak[...] = jnp.broadcast_to(top, (8, 128))
        mass[...] = jnp.broadcast_to(jnp.sum(total, axis=1, keepdims=True), (8, 128))
        post[...] = total + pltpu.roll(total, CPAD, 1)

def match(wt, refs, ctf, classes):
    fwd, bwd = rotation_coefs()
    small = jax.ShapeDtypeStruct((8, 128), F32)
    whole = pl.BlockSpec(memory_space=pltpu.VMEM)
    return pl.pallas_call(
        functools.partial(match_kernel, classes),
        grid=(ANGLES // ROTS,),
        out_shape=(jax.ShapeDtypeStruct((FOLD, QROWS, 128), F32), small, small, small),
        in_specs=[pl.BlockSpec((ROTS, QROWS, 256), lambda d: (d, 0, 0)),
                  pl.BlockSpec((4, 2, 9, CPAD, 128), lambda d: (d, 0, 0, 0, 0)), whole, whole, whole],
        out_specs=(whole,) * 4,
        scratch_shapes=[pltpu.VMEM((FOLD, QROWS, 128), F32), pltpu.VMEM((128, 128), F32)],
        compiler_params=pltpu.CompilerParams(vmem_limit_bytes=48 * 2**20),
        name="match",
    )(wt, refs, ctf, jnp.asarray(fwd), jnp.asarray(bwd))

COMBOS = [(ry, c) for ry in (1, 0) for c in (2, 1, 3, 0)]
BLOCKS = [(2, 1), (2, 0), (1, 1), (3, 1), (1, 0), (3, 0), (0, 1), (0, 0)]
BLOCK_UNITS = 0.6


def scatter_plan():
    links, steps, got, done = Links(), [], set(), set()

    def send(t, half, stage, combo, kind):
        axis = axes_of(half)[::-1][stage]
        sign = 1 if kind in ("a0", "l0", "l1", "y") else -1
        size = 1.0 if kind == "y" else SUB[int(kind[1])] / sum(SUB)
        msg = (half, stage, combo, kind)
        steps.append((t, "send", msg))
        links.send(t, axis, sign, size, msg)

    def have(half, stage, combo, k):
        if stage == 2:
            return (half, 2, k) in done
        return ((k, combo[0]) if half == 0 else (combo[1], combo[0])) in done

    def ready(t, half, stage, combo, k):
        if k == 2:
            send(t, half, stage, combo, "a0")
            send(t, half, stage, combo, "a1")
        elif k == 1:
            send(t, half, stage, combo, "l1")
            relay(t, half, stage, combo, "a0")
        elif k == 3:
            send(t, half, stage, combo, "r0")
            relay(t, half, stage, combo, "a1")
        else:
            total(t, half, stage, combo)

    def relay(t, half, stage, combo, kind):
        k = 1 if kind == "a0" else 3
        if (half, stage, combo, kind) in got and have(half, stage, combo, k):
            steps.append((t, "relay", (half, stage, combo, kind)))
            send(t, half, stage, combo, "l0" if kind == "a0" else "r1")

    def total(t, half, stage, combo):
        kinds = ("l0", "l1", "r0", "r1")
        if all((half, stage, combo, kind) in got for kind in kinds) and have(half, stage, combo, 0):
            steps.append((t, "total", (half, stage, combo)))
            if stage == 0:
                done.add((half, 0, combo, "s"))
                if combo[0] == 1:
                    send(t, half, 1, combo[1], "y")
                else:
                    second(t, half, combo[1])

    def second(t, half, c):
        if (half, 0, (0, c), "s") in done and (half, 1, c, "y") in got:
            steps.append((t, "pair", (half, c)))
            done.add((half, 2, c))
            ready(t, half, 2, None, c)

    for i, block in enumerate(BLOCKS):
        links.push((i + 1) * BLOCK_UNITS, ("block", block))
    while links.heap:
        t, key = links.pop()
        if key[0] == "block":
            z, y = key[1]
            done.add((z, y))
            for x in (2, 1, 3, 0):
                ready(t, 0, 0, (y, x), z)
                ready(t, 1, 0, (y, z), x)
            continue
        half, stage, combo, kind = key
        steps.append((t, "wait", key))
        got.add(key)
        if kind == "y":
            second(t, half, combo)
        elif kind in ("a0", "a1"):
            relay(t, half, stage, combo, kind)
        else:
            total(t, half, stage, combo)
    return steps


def scatter_keys():
    steps = scatter_plan()
    return steps, {s[2]: i for i, s in enumerate(s for s in steps if s[1] == "send")}


class Scatter:
    def __init__(self, me, own, three, pair, out, send_sem, recv_sem):
        self.me, self.own, self.three, self.pair, self.out = me, own, three, pair, out
        self.send_sem, self.recv_sem = send_sem, recv_sem
        self.steps, self.index = scatter_keys()
        self.sent = []

    def group(self, stage, combo):
        return 8 if stage == 2 else COMBOS.index(combo)

    def mine(self, half, stage, combo, k):
        if stage == 2:
            return self.pair.at[half, k]
        order = axes_of(half)[::-1]
        rel = [0, 0, 0]
        rel[order[0]] = k
        rel[1] = combo[0]
        rel[order[2]] = combo[1]
        return self.own.at[slot(self.me, rel), half]

    def box(self, msg):
        half, stage, combo, kind = msg
        if kind == "y":
            return self.pair.at[half, combo]
        which = {"a": 0, "l": 1, "r": 2}[kind[0]]
        return self.three.at[half, self.group(stage, combo), which, span(int(kind[1]))]

    def source(self, msg):
        half, stage, combo, kind = msg
        if kind == "y":
            return self.three.at[half, self.group(0, (1, combo)), 1]
        where = span(int(kind[1]))
        if kind in ("a0", "a1"):
            return self.mine(half, stage, combo, 2).at[where]
        if kind == "l1":
            return self.mine(half, stage, combo, 1).at[where]
        if kind == "r0":
            return self.mine(half, stage, combo, 3).at[where]
        return self.three.at[half, self.group(stage, combo), 0, where]

    def copy(self, msg, src=None):
        half, stage, combo, kind = msg
        axis = axes_of(half)[::-1][stage]
        sign = 1 if kind in ("a0", "l0", "l1", "y") else -1
        i = self.index[msg]
        box = self.box(msg)
        return pltpu.make_async_remote_copy(
            src_ref=box if src is None else src,
            dst_ref=box,
            send_sem=self.send_sem.at[i],
            recv_sem=self.recv_sem.at[i],
            device_id=peer(self.me, toward(axis, sign)),
            device_id_type=MESH,
        )

    def add(self, dst, terms, count):
        def one(i, carry):
            value = terms[0][i].astype(F32)
            for term in terms[1:]:
                value = value + term[i].astype(F32)
            dst[i] = value.astype(dst.dtype)
            return carry

        lax.fori_loop(0, count, one, 0)

    def step(self, item):
        _, what, key = item
        if what == "send":
            self.copy(key, self.source(key)).start()
            self.sent.append(key)
        elif what == "wait":
            self.copy(key).wait_recv()
        elif what == "relay":
            half, stage, combo, kind = key
            box = self.box(key)
            mine = self.mine(half, stage, combo, 1 if kind == "a0" else 3).at[span(int(kind[1]))]
            self.add(box, (mine, box), SUB[int(kind[1])])
        elif what == "pair":
            half, c = key
            box = self.pair.at[half, c]
            self.add(box, (self.three.at[half, self.group(0, (0, c)), 1], box), sum(SUB))
        else:
            half, stage, combo = key
            left = self.three.at[half, self.group(stage, combo), 1]
            right = self.three.at[half, self.group(stage, combo), 2]
            mine = self.mine(half, stage, combo, 0)
            dst = self.out.at[half] if stage == 2 else left
            self.add(dst, (mine, left, right), sum(SUB))

    def finish(self):
        for key in self.sent:
            self.copy(key, self.source(key)).wait_send()


def back_kernel(wt, spec, stat, out, logz, own, three, pair, tab, seen, send_sem, recv_sem, stat_send, stat_recv):
    i = pl.program_id(0)
    me = place()
    x, y, z, cls = me
    work = Scatter(me, own, three, pair, out, send_sem, recv_sem)
    last = len(BLOCKS) - 1
    due = {}
    for item in work.steps:
        at = min(last, max(0, math.ceil(item[0] / BLOCK_UNITS - 0.001) - 1))
        due.setdefault(at, []).append(item)

    @pl.when(i == 0)
    def _():
        dp = slot(me, (0, 0, 0))
        barrier = pltpu.get_barrier_semaphore()
        there = [peer(me, toward(*move)) for move in ((0, 1), (0, -1), (1, 1), (2, 1), (2, -1))]
        others = [(dp, (cls + k) % 4) for k in (1, 2, 3)]
        for device in there + others:
            pl.semaphore_signal(barrier, inc=1, device_id=device, device_id_type=MESH)
        pl.semaphore_wait(barrier, len(there) + len(others))
        copies = []
        for k, device in enumerate(others):
            copy = pltpu.make_async_remote_copy(
                src_ref=stat,
                dst_ref=seen.at[k],
                send_sem=stat_send.at[k],
                recv_sem=stat_recv.at[k],
                device_id=device,
                device_id_type=MESH,
            )
            copy.start()
            copies.append(copy)
        for copy in copies:
            copy.wait()
        peaks = [stat[0]] + [seen[k, 0] for k in range(3)]
        masses = [stat[1]] + [seen[k, 1] for k in range(3)]
        top = jnp.maximum(jnp.maximum(peaks[0], peaks[1]), jnp.maximum(peaks[2], peaks[3]))
        mass = masses[0] * jnp.exp(peaks[0] - top)
        for k in range(1, 4):
            mass = mass + masses[k] * jnp.exp(peaks[k] - top)
        total = top + jnp.log(mass)
        logz[...] = total
        scale = jnp.concatenate([jnp.exp(peaks[0] - total)] * (QROWS // 8), 0)
        for g in range(FOLD):
            tab[g] = (spec[g] * scale).T.astype(BF16)

    dz = jnp.int32(0)
    dy = jnp.int32(0)
    for at, (bz, by) in enumerate(BLOCKS):
        dz = jnp.where(i == at, bz, dz)
        dy = jnp.where(i == at, by, dy)
    base = (((z + dz) % 4) * 2 + (y + dy) % 2) * 4
    for r in range(ROTS):
        g, sg = fold_of(r)
        both = jnp.dot(tab[g], wt[r], preferred_element_type=F32)
        a, b = both[:CPAD], both[CPAD:]
        own[base + r // 9, 0, r % 9] = (a[:, :128] - sg * b[:, 128:]).astype(BF16)
        own[base + r // 9, 1, r % 9] = (a[:, 128:] + sg * b[:, :128]).astype(BF16)

    for at in range(len(BLOCKS)):

        @pl.when(i == at)
        def _(at=at):
            for item in due.get(at, []):
                work.step(item)
            if at == last:
                work.finish()


def block_index(i):
    dp = lax.axis_index("dp")
    dz = jnp.int32(0)
    dy = jnp.int32(0)
    for at, (bz, by) in enumerate(BLOCKS):
        dz = jnp.where(i == at, bz, dz)
        dy = jnp.where(i == at, by, dy)
    return ((dp // 8 + dz) % 4) * 2 + ((dp // 4) % 2 + dy) % 2, 0, 0


def back(wt, spec, stat):
    steps, index = scatter_keys()
    whole = pl.BlockSpec(memory_space=pltpu.VMEM)
    owners = SIZES[0] * SIZES[1] * SIZES[2]
    block = (ANGLES // owners, CPAD, 128)
    return pl.pallas_call(
        back_kernel,
        grid=(len(BLOCKS),),
        out_shape=(jax.ShapeDtypeStruct((2,) + block, F32), jax.ShapeDtypeStruct((8, 128), F32)),
        in_specs=[pl.BlockSpec((ROTS, QROWS, 256), block_index), whole, whole],
        out_specs=(whole, whole),
        scratch_shapes=[
            pltpu.VMEM((owners, 2) + block, BF16),
            pltpu.VMEM((2, 9, 3) + block, BF16),
            pltpu.VMEM((2, 4) + block, BF16),
            pltpu.VMEM((FOLD, 128, QROWS), BF16),
            pltpu.VMEM((3, 2, 8, 128), F32),
            pltpu.SemaphoreType.DMA((len(index),)),
            pltpu.SemaphoreType.DMA((len(index),)),
            pltpu.SemaphoreType.DMA((3,)),
            pltpu.SemaphoreType.DMA((3,)),
        ],
        compiler_params=pltpu.CompilerParams(
            collective_id=2, has_side_effects=True, vmem_limit_bytes=48 * 2**20
        ),
        name="back",
    )(wt, spec, stat)


def twist_tables(freq, rot_offset):
    idx = (freq[:, None] * rot_offset[None, :]) % ANGLES
    rad = idx.astype(F32) * (2.0 * math.pi / ANGLES)
    return jnp.cos(rad)[:, :, None], jnp.sin(rad)[:, :, None]


def twist_refs(references, cos, sin):
    re = references[:, 0].astype(F32)
    im = references[:, 1].astype(F32)
    both = jnp.stack([re * cos + im * sin, im * cos - re * sin], 1)
    both = jnp.pad(both, ((0, 0), (0, 0), (0, CPAD - both.shape[2]), (0, 0))).astype(BF16)
    both = both.reshape(both.shape[0], 2 * CPAD, 2, 64)
    return jnp.transpose(both, (2, 0, 3, 1))


def untwist(sums, cos, sin, classes):
    re = sums[0, :, :classes].astype(F32)
    im = sums[1, :, :classes].astype(F32)
    return jnp.stack([re * cos - im * sin, re * sin + im * cos], 1)


def order_angles(particles):
    return jnp.concatenate([particles[:, :, 0::2], particles[:, :, 1::2]], 2)


def group_rows(defocus_group, ctf_table):
    hit = defocus_group[:, None] == jnp.arange(ctf_table.shape[0], dtype=jnp.int32)[None, :]
    return jnp.sum(jnp.where(hit[:, :, None], ctf_table[None], 0.0), 1)


def local(particles, references, ctf_table, rot_offset, prior_shift, defocus_group):
    block, _, classes = references.shape[:3]
    freq = lax.axis_index("dp") * block + jnp.arange(block, dtype=jnp.int32)
    cos, sin = twist_tables(freq, rot_offset)
    ctf = group_rows(defocus_group, ctf_table)
    wt, refs = transform(prior_shift, order_angles(particles), ctf, twist_refs(references, cos, sin))
    spec, peak, mass, post = match(wt, refs, ctf, classes)
    sums, total = back(wt, spec, jnp.stack([peak, mass]))
    posterior = post[:, :classes] * jnp.exp(peak[:, :classes] - total[:, :classes])
    return total[:, 0], posterior, untwist(sums, cos, sin, classes)


def solution(mesh):
    placed = (
        P("dp", None, None, None),
        P("dp", None, "cls", None),
        P(),
        P("cls"),
        P("dp", None),
        P("dp"),
    )
    return jax.shard_map(
        local,
        mesh=mesh,
        in_specs=placed,
        out_specs=(P("dp"), P("dp", "cls"), P("dp", None, "cls", None)),
        check_vma=False,
    )
```

```python
import functools
import heapq
import math

import jax
import jax.numpy as jnp
import numpy as np
from jax import lax
from jax.experimental import pallas as pl
from jax.experimental.pallas import tpu as pltpu
from jax.sharding import PartitionSpec as P

ROTS = 36
SIDE = 5
SHIFTS = SIDE * SIDE
ANGLES = 288
CYCLES = 128
HALF = ANGLES // 2
REACH = 10
FOLD = ROTS // 2 + 1
IPAD = 80
QROWS = 208
CPAD = 64
F32 = jnp.float32
BF16 = jnp.bfloat16
MESH = pl.DeviceIdType.MESH


def phase_tables():
    order = np.concatenate([np.arange(0, ANGLES, 2), np.arange(1, ANGLES, 2)])
    theta = 2.0 * np.pi * order / ANGLES
    radius = (np.arange(CYCLES) + 1) / (2.0 * CYCLES)
    count = np.arange(REACH + 1)
    out = []
    for wave in (np.cos(theta), np.sin(theta)):
        arg = 2.0 * np.pi * count[:, None, None] * wave[None, :, None] * radius[None, None, :]
        out.append(np.stack([np.cos(arg), np.sin(arg)], 1).astype(np.float32))
    return out


def dft_tables():
    row = np.arange(IPAD)
    out = []
    for start in (0, 1):
        t = np.arange(start, ANGLES, 2)
        ang = 2.0 * np.pi * ((row[:, None] * t[None, :]) % ANGLES) / ANGLES
        out.append(np.concatenate([np.cos(ang), np.sin(ang)], 0).astype(np.float32))
    return out


def rotation_coefs():
    k = np.arange(FOLD)
    ang = 2.0 * np.pi * ((k[:, None] * k[None, :]) % ROTS) / ROTS
    cos, sin = np.cos(ang), np.sin(ang)
    lanes = np.arange(128) < CPAD
    fwd = np.where(lanes, cos[:, :, None], -sin[:, :, None]) / ANGLES
    bwd = np.where(lanes, cos[:, :, None], sin[:, :, None])
    return fwd.astype(np.float32), bwd.astype(np.float32)


SIZES = (4, 2, 4)
TILES = 57
PARTS = ((0, 15, 29), (29, 43, 57))
LATE = 0.35


def place():
    dp = lax.axis_index("dp")
    return dp % 4, (dp // 4) % 2, dp // 8, lax.axis_index("cls")


def peer(me, rel):
    x, y, z, cls = me
    return ((((z + rel[2]) % 4) * 2 + (y + rel[1]) % 2) * 4 + (x + rel[0]) % 4, cls)


def slot(me, rel):
    return peer(me, rel)[0]


def toward(axis, sign):
    move = [0, 0, 0]
    move[axis] = sign
    return tuple(move)


def greet(me):
    barrier = pltpu.get_barrier_semaphore()
    moves = [toward(0, 1), toward(0, -1), toward(1, 1), toward(2, 1), toward(2, -1)]
    for move in moves:
        pl.semaphore_signal(barrier, inc=1, device_id=peer(me, move), device_id_type=MESH)
    pl.semaphore_wait(barrier, len(moves))


def axes_of(half):
    return (0, 1, 2) if half == 0 else (2, 1, 0)


def span(half, sub):
    low, mid, high = PARTS[half]
    first, end = ((low, high), (low, mid), (mid, high))[0 if sub is None else sub + 1]
    return pl.ds(first, end - first)


def share(half, sub):
    low, mid, high = PARTS[half]
    return ((high - low) if sub is None else (mid - low, high - mid)[sub]) * 2.0 / TILES


class Links:
    def __init__(self):
        self.free, self.heap, self.count = {}, [], 0

    def send(self, t, axis, sign, size, key):
        start = max(t, self.free.get((axis, sign), 0.0))
        self.free[(axis, sign)] = start + size
        self.push(start + size + LATE, key)

    def push(self, t, key):
        self.count += 1
        heapq.heappush(self.heap, (t, self.count, key))

    def pop(self):
        t, _, key = heapq.heappop(self.heap)
        return t, key


def gather_plan():
    links, plan, got = Links(), [], {}
    for half in (0, 1):
        links.push(0.0, (half, (0, 0, 0), None))
    while links.heap:
        t, key = links.pop()
        half, rel, sub = key
        order = axes_of(half)
        sends = []

        def go(axis, sign, sub):
            seen = list(rel)
            seen[axis] = (seen[axis] - sign) % SIZES[axis]
            there = (half, tuple(seen), sub)
            sends.append((half, rel, sub, axis, sign, there))
            links.send(t, axis, sign, share(half, sub), there)

        got[half, rel] = got.get((half, rel), 0) + 1
        if sub is None or got[half, rel] == 2:
            last = max([i for i in range(3) if rel[order[i]]], default=-1)
            for i in range(2, last, -1):
                if order[i] == 1:
                    go(1, 1, None)
                else:
                    go(order[i], 1, None)
                    go(order[i], -1, None)
            if last >= 0 and order[last] != 1:
                if rel[order[last]] == 3:
                    go(order[last], 1, 0)
                elif rel[order[last]] == 1:
                    go(order[last], -1, 1)
        plan.append((t, None if rel == (0, 0, 0) else key, sends))
    return plan


def gather_keys():
    plan = gather_plan()
    recv = {step[1]: i for i, step in enumerate(s for s in plan if s[1] is not None)}
    return plan, recv


class Gather:
    def __init__(self, me, own, store, send_sem, recv_sem):
        self.me, self.own, self.store = me, own, store
        self.send_sem, self.recv_sem = send_sem, recv_sem
        self.plan, self.recv = gather_keys()
        self.sent = []

    def copy(self, index, half, rel, sub, axis, sign, there):
        where = span(half, sub)
        here = self.own.at[where] if rel == (0, 0, 0) else self.store.at[slot(self.me, rel), where]
        return pltpu.make_async_remote_copy(
            src_ref=here,
            dst_ref=self.store.at[slot(self.me, rel), where],
            send_sem=self.send_sem.at[index],
            recv_sem=self.recv_sem.at[self.recv[there]],
            device_id=peer(self.me, toward(axis, sign)),
            device_id_type=MESH,
        )

    def arrived(self, key):
        half, rel, sub = key
        here = self.store.at[slot(self.me, rel), span(half, sub)]
        pltpu.make_async_remote_copy(
            src_ref=here,
            dst_ref=here,
            send_sem=self.send_sem.at[0],
            recv_sem=self.recv_sem.at[self.recv[key]],
            device_id=peer(self.me, (1, 0, 0)),
            device_id_type=MESH,
        ).wait_recv()

    def step(self, item):
        _, key, sends = item
        if key is not None:
            self.arrived(key)
        for send in sends:
            self.copy(len(self.sent), *send).start()
            self.sent.append(send)

    def finish(self):
        for index, send in enumerate(self.sent):
            self.copy(index, *send).wait_send()


GROUP = 8
STEPS = 26
PITCH = 4 * IPAD + 1
UNIT_STEPS = 2.06


def transform_kernel(shift, group, part, ctf, txh, tyh, te, to, own, out, store, tx, ty, z1, xs, fr, fi, send_sem, recv_sem, own_sem, tab_sem):
    u = pl.program_id(0)
    me = place()
    work = Gather(me, own, store, send_sem, recv_sem)
    keep = pltpu.make_async_copy(own, store.at[slot(me, (0, 0, 0))], own_sem)
    due = {}
    for item in work.plan:
        at = 0 if item[1] is None else min(STEPS - 1, math.ceil(item[0] * UNIT_STEPS))
        due.setdefault(at, []).append(item)

    loads = [pltpu.make_async_copy(txh, tx, tab_sem.at[0]), pltpu.make_async_copy(tyh, ty, tab_sem.at[1])]

    @pl.when(u == 0)
    def _():
        for load in loads:
            load.start()
        greet(me)
        keep.start()

    for at in sorted(due):
        if at < STEPS - 1:

            @pl.when(u == at)
            def _(at=at):
                for item in due[at]:
                    work.step(item)

    @pl.when(u == 0)
    def _():
        for load in loads:
            load.wait()

    s = jnp.minimum(u, SHIFTS - 1)
    a = s // SIDE
    b = s % SIDE

    @pl.when((b == 0) & (u < SHIFTS))
    def _():
        def ramp(p, carry):
            sx = shift[p, 0] + a - SIDE // 2
            n = jnp.abs(sx)
            sg = jnp.where(sx < 0, -1.0, 1.0).astype(F32)
            for c in range(0, ANGLES, 48):
                rows = pl.ds(c, 48)
                re = part[p, 0, rows, :].astype(F32)
                im = part[p, 1, rows, :].astype(F32)
                co = tx[n, 0, rows, :]
                si = tx[n, 1, rows, :] * sg
                z1[p, 0, rows, :] = re * co + im * si
                z1[p, 1, rows, :] = im * co - re * si
            return carry

        lax.fori_loop(0, GROUP, ramp, 0)

    @pl.when(u < SHIFTS)
    def _():
        for p in range(GROUP):
            sy = shift[p, 1] + b - SIDE // 2
            n = jnp.abs(sy)
            sg = jnp.where(sy < 0, -1.0, 1.0).astype(F32)
            for c in range(0, ANGLES, 16):
                rows = pl.ds(c, 16)
                re = z1[p, 0, rows, :]
                im = z1[p, 1, rows, :]
                co = ty[n, 0, rows, :]
                si = ty[n, 1, rows, :] * sg
                xs[rows, 256 * p : 256 * p + 128] = (re * co + im * si).astype(BF16)
                xs[rows, 256 * p + 128 : 256 * p + 256] = (im * co - re * si).astype(BF16)
        even = jnp.dot(te[...], xs[0:HALF, :], preferred_element_type=F32)
        odd = jnp.dot(to[...], xs[HALF:, :], preferred_element_type=F32)
        for p in range(GROUP):
            j = (u % 2) * GROUP + p
            gain = ctf[pl.ds(group[p], 1), :]
            lo, hi = slice(256 * p, 256 * p + 128), slice(256 * p + 128, 256 * p + 256)
            for c in range(0, IPAD, 8):
                cos, sin = slice(c, c + 8), slice(IPAD + c, IPAD + c + 8)
                u1 = (even[cos, lo] + even[sin, hi]) * gain
                u2 = (even[cos, lo] - even[sin, hi]) * gain
                w1 = (even[cos, hi] - even[sin, lo]) * gain
                w2 = (even[cos, hi] + even[sin, lo]) * gain
                v1 = (odd[cos, lo] + odd[sin, hi]) * gain
                v2 = (odd[cos, lo] - odd[sin, hi]) * gain
                y1 = (odd[cos, hi] - odd[sin, lo]) * gain
                y2 = (odd[cos, hi] + odd[sin, lo]) * gain
                for blk, (re, im) in enumerate(
                    ((u1 + v1, w1 + y1), (u1 - v1, w1 - y1), (u2 - v2, w2 - y2), (u2 + v2, w2 + y2))
                ):
                    rows = pl.ds(j * PITCH + blk * IPAD + c, 8)
                    fr[rows, :] = re
                    fi[rows, :] = im

    def emit(i, blk, m):
        rows = pl.ds(blk * IPAD + i, 2 * GROUP, stride=PITCH)
        out[m, :, 0:128] = fr[rows, :].astype(BF16)
        out[m, :, 128:256] = fi[rows, :].astype(BF16)

    @pl.when(u % 2 == 1)
    def _():
        def pack(i, carry):
            emit(i, 0, i)
            emit(i, 1, HALF + i)
            emit(i, 2, HALF - i)
            emit(i, 3, ANGLES - i)
            return carry

        emit(0, 0, 0)
        emit(0, 1, HALF)
        emit(HALF // 2, 0, HALF // 2)
        emit(HALF // 2, 1, HALF + HALF // 2)
        lax.fori_loop(1, HALF // 2, pack, 0, unroll=8)

    @pl.when(u == STEPS - 1)
    def _():
        for item in due.get(STEPS - 1, []):
            work.step(item)
        keep.wait()
        work.finish()


def transform(shift, group, part, ctf, own):
    tx, ty = phase_tables()
    te, to = dft_tables()
    plan, recv = gather_keys()
    whole = pl.BlockSpec(memory_space=pltpu.VMEM)
    near = pl.BlockSpec(memory_space=pltpu.SMEM)
    far = pl.BlockSpec(memory_space=pl.ANY)
    owners = SIZES[0] * SIZES[1] * SIZES[2]
    return pl.pallas_call(
        transform_kernel,
        grid=(STEPS,),
        out_shape=(
            jax.ShapeDtypeStruct((ANGLES, QROWS, 256), BF16),
            jax.ShapeDtypeStruct((owners,) + own.shape, own.dtype),
        ),
        in_specs=[near, near, whole, whole, far, far, whole, whole, whole],
        out_specs=(
            pl.BlockSpec((ANGLES, 2 * GROUP, 256), lambda u: (0, u // 2, 0)),
            pl.BlockSpec(memory_space=pl.ANY),
        ),
        scratch_shapes=[
            pltpu.VMEM((REACH + 1, 2, ANGLES, 128), F32),
            pltpu.VMEM((REACH + 1, 2, ANGLES, 128), F32),
            pltpu.VMEM((GROUP, 2, ANGLES, 128), F32),
            pltpu.VMEM((ANGLES, 256 * GROUP), BF16),
            pltpu.VMEM((2 * GROUP * PITCH + 8, 128), F32),
            pltpu.VMEM((2 * GROUP * PITCH + 8, 128), F32),
            pltpu.SemaphoreType.DMA((sum(len(s[2]) for s in plan),)),
            pltpu.SemaphoreType.DMA((len(recv),)),
            pltpu.SemaphoreType.DMA,
            pltpu.SemaphoreType.DMA((2,)),
        ],
        compiler_params=pltpu.CompilerParams(
            collective_id=1, has_side_effects=True, vmem_limit_bytes=56 * 2**20
        ),
        name="transform",
    )(shift, group, part, ctf, jnp.asarray(tx), jnp.asarray(ty), jnp.asarray(te, BF16), jnp.asarray(to, BF16), own)


H = FOLD // 2
HALF_ROWS = TILES * 8

def fold_of(r):
    return (r, 1) if r <= ROTS // 2 else (ROTS - r, -1)

def half_sums(parts, tab, k):
    even = parts[0] * tab[k, 0:1, :]
    for g in range(2, FOLD, 2):
        even = even + parts[g] * tab[k, g : g + 1, :]
    odd = parts[1] * tab[k, 1:2, :]
    for g in range(3, FOLD, 2):
        odd = odd + parts[g] * tab[k, g : g + 1, :]
    return even, odd

def match_kernel(classes, group, wt, refs, ctf, fwd, bwd, spec, peak, mass, post, acc, power, flat):
    d = pl.program_id(0)
    first = d == 0
    for o in range(4):
        flat[o, 0 : TILES * 16] = refs[o].reshape(TILES * 16, 128).astype(F32)

    def image(r, part):
        at = part * HALF_ROWS + (r % 9) * classes
        return flat[r // 9, pl.ds(at, CPAD), :]

    def product(r, squares):
        re, im = image(r, 0), image(r, 1)
        squares.append(re * re + im * im)
        re, im = re.astype(BF16), im.astype(BF16)
        if fold_of(r)[1] > 0:
            table = jnp.concatenate([jnp.concatenate([re, im], 1), jnp.concatenate([-im, re], 1)], 0)
        else:
            table = jnp.concatenate([jnp.concatenate([re, im], 1), jnp.concatenate([im, -re], 1)], 0)
        return lax.dot_general(wt[r], table, (((1,), (1,)), ((), ())), preferred_element_type=F32)

    @pl.when(first)
    def _():
        acc[...] = jnp.zeros_like(acc)
        power[...] = jnp.zeros_like(power)
        flat[:, TILES * 16 :] = jnp.zeros((4, 8, 128), F32)

    pw = power[...]
    for g in range(FOLD):
        squares = []
        y = product(g, squares)
        if 0 < g < FOLD - 1:
            y = y + product(ROTS - g, squares)
        acc[g] += y
        for term in squares:
            pw = pw + term
    power[...] = pw

    @pl.when(d == pl.num_programs(0) - 1)
    def _():
        gain = jnp.concatenate([ctf[pl.ds(group[p], 1), :] for p in range(8)], 0)
        half = lax.dot_general(
            gain * gain,
            power[...],
            (((1,), (1,)), ((), ())),
            precision=lax.Precision.HIGHEST,
            preferred_element_type=F32,
        ) * (0.5 / ANGLES)
        bias = jnp.concatenate([half, half], 1)
        lane = lax.broadcasted_iota(jnp.int32, (8, 128), 1)
        live = lane % CPAD < classes
        edge = lane < classes
        sign = jnp.where(lane < CPAD, 1.0, -1.0).astype(F32)
        low = -1e30

        def score(s, top):
            rows = pl.ds(pl.multiple_of(s * 8, 8), 8)
            parts = [acc[g, rows, :] for g in range(FOLD)]
            for k in range(H + 1):
                even, odd = half_sums(parts, fwd, k)
                y, w = even + odd, even - odd
                both = [(k, y * sign + pltpu.roll(y, CPAD, 1))]
                if k < H:
                    both.append((FOLD - 1 - k, w + pltpu.roll(w * sign, CPAD, 1)))
                for at, z in both:
                    z = z - bias
                    z = jnp.where(edge if at in (0, FOLD - 1) else live, z, low)
                    spec[at, rows, :] = z
                    top = jnp.maximum(top, z)
            return top

        top = lax.fori_loop(0, SHIFTS, score, jnp.full((8, 128), low, F32), unroll=5)
        top = jnp.max(top, axis=1, keepdims=True)

        def weigh(s, total):
            rows = pl.ds(pl.multiple_of(s * 8, 8), 8)
            parts = []
            for k in range(FOLD):
                e = jnp.exp(spec[k, rows, :] - top)
                total = total + e
                parts.append(e * sign + pltpu.roll(e, CPAD, 1))
            for g in range(H + 1):
                even, odd = half_sums(parts, bwd, g)
                spec[g, rows, :] = even + odd
                if g < H:
                    spec[FOLD - 1 - g, rows, :] = (even - odd) * sign
            return total

        total = lax.fori_loop(0, SHIFTS, weigh, jnp.zeros((8, 128), F32), unroll=5)
        spec[:, SHIFTS * 8 :, :] = jnp.zeros((FOLD, QROWS - SHIFTS * 8, 128), F32)
        peak[...] = jnp.broadcast_to(top, (8, 128))
        mass[...] = jnp.broadcast_to(jnp.sum(total, axis=1, keepdims=True), (8, 128))
        post[...] = total + pltpu.roll(total, CPAD, 1)

def match(group, wt, refs, ctf, classes):
    fwd, bwd = rotation_coefs()
    small = jax.ShapeDtypeStruct((8, 128), F32)
    whole = pl.BlockSpec(memory_space=pltpu.VMEM)
    return pl.pallas_call(
        functools.partial(match_kernel, classes),
        grid=(ANGLES // ROTS,),
        out_shape=(jax.ShapeDtypeStruct((FOLD, QROWS, 128), F32), small, small, small),
        in_specs=[pl.BlockSpec(memory_space=pltpu.SMEM), pl.BlockSpec((ROTS, QROWS, 256), lambda d: (d, 0, 0)),
                  pl.BlockSpec((4, TILES, 16, 128), lambda d: (d, 0, 0, 0)), whole, whole, whole],
        out_specs=(whole,) * 4,
        scratch_shapes=[pltpu.VMEM((FOLD, QROWS, 128), F32), pltpu.VMEM((CPAD, 128), F32), pltpu.VMEM((4, TILES * 16 + 8, 128), F32)],
        compiler_params=pltpu.CompilerParams(vmem_limit_bytes=48 * 2**20),
        name="match",
    )(group, wt, refs, ctf, jnp.asarray(fwd), jnp.asarray(bwd))

COMBOS = [(ry, c) for ry in (1, 0) for c in (2, 1, 3, 0)]
BLOCKS = [(2, 1), (2, 0), (1, 1), (3, 1), (1, 0), (3, 0), (0, 1), (0, 0)]
BLOCK_UNITS = 0.6


def scatter_plan():
    links, steps, got, done = Links(), [], set(), set()

    def send(t, half, stage, combo, kind):
        axis = axes_of(half)[::-1][stage]
        sign = 1 if kind in ("a0", "l0", "l1", "y") else -1
        size = share(half, None if kind == "y" else int(kind[1]))
        msg = (half, stage, combo, kind)
        steps.append((t, "send", msg))
        links.send(t, axis, sign, size, msg)

    def have(half, stage, combo, k):
        if stage == 2:
            return (half, 2, k) in done
        return ((k, combo[0]) if half == 0 else (combo[1], combo[0])) in done

    def ready(t, half, stage, combo, k):
        if k == 2:
            send(t, half, stage, combo, "a0")
            send(t, half, stage, combo, "a1")
        elif k == 1:
            send(t, half, stage, combo, "l1")
            relay(t, half, stage, combo, "a0")
        elif k == 3:
            send(t, half, stage, combo, "r0")
            relay(t, half, stage, combo, "a1")
        else:
            total(t, half, stage, combo)

    def relay(t, half, stage, combo, kind):
        k = 1 if kind == "a0" else 3
        if (half, stage, combo, kind) in got and have(half, stage, combo, k):
            steps.append((t, "relay", (half, stage, combo, kind)))
            send(t, half, stage, combo, "l0" if kind == "a0" else "r1")

    def total(t, half, stage, combo):
        kinds = ("l0", "l1", "r0", "r1")
        if all((half, stage, combo, kind) in got for kind in kinds) and have(half, stage, combo, 0):
            steps.append((t, "total", (half, stage, combo)))
            if stage == 0:
                done.add((half, 0, combo, "s"))
                if combo[0] == 1:
                    send(t, half, 1, combo[1], "y")
                else:
                    second(t, half, combo[1])

    def second(t, half, c):
        if (half, 0, (0, c), "s") in done and (half, 1, c, "y") in got:
            steps.append((t, "pair", (half, c)))
            done.add((half, 2, c))
            ready(t, half, 2, None, c)

    for i, block in enumerate(BLOCKS):
        links.push((i + 1) * BLOCK_UNITS, ("block", block))
    while links.heap:
        t, key = links.pop()
        if key[0] == "block":
            z, y = key[1]
            done.add((z, y))
            for x in (2, 1, 3, 0):
                ready(t, 0, 0, (y, x), z)
                ready(t, 1, 0, (y, z), x)
            continue
        half, stage, combo, kind = key
        steps.append((t, "wait", key))
        got.add(key)
        if kind == "y":
            second(t, half, combo)
        elif kind in ("a0", "a1"):
            relay(t, half, stage, combo, kind)
        else:
            total(t, half, stage, combo)
    return steps


def scatter_keys():
    steps = scatter_plan()
    return steps, {s[2]: i for i, s in enumerate(s for s in steps if s[1] == "send")}


def inner(half, sub):
    low, mid, high = PARTS[half]
    first, end = ((low, high), (low, mid), (mid, high))[0 if sub is None else sub + 1]
    return pl.ds(first - low, end - first)


class Scatter:
    def __init__(self, me, own, three, pair, out, send_sem, recv_sem):
        self.me, self.own, self.three, self.pair, self.out = me, own, three, pair, out
        self.send_sem, self.recv_sem = send_sem, recv_sem
        self.steps, self.index = scatter_keys()
        self.sent = []

    def group(self, stage, combo):
        return 8 if stage == 2 else COMBOS.index(combo)

    def mine(self, half, stage, combo, k, sub=None):
        if stage == 2:
            return self.pair.at[half, k, inner(half, sub)]
        order = axes_of(half)[::-1]
        rel = [0, 0, 0]
        rel[order[0]] = k
        rel[1] = combo[0]
        rel[order[2]] = combo[1]
        return self.own.at[slot(self.me, rel), span(half, sub)]

    def box(self, msg):
        half, stage, combo, kind = msg
        if kind == "y":
            return self.pair.at[half, combo, inner(half, None)]
        which = {"a": 0, "l": 1, "r": 2}[kind[0]]
        return self.three.at[half, self.group(stage, combo), which, inner(half, int(kind[1]))]

    def source(self, msg):
        half, stage, combo, kind = msg
        if kind == "y":
            return self.three.at[half, self.group(0, (1, combo)), 1, inner(half, None)]
        sub = int(kind[1])
        if kind in ("a0", "a1"):
            return self.mine(half, stage, combo, 2, sub)
        if kind == "l1":
            return self.mine(half, stage, combo, 1, sub)
        if kind == "r0":
            return self.mine(half, stage, combo, 3, sub)
        return self.three.at[half, self.group(stage, combo), 0, inner(half, sub)]

    def copy(self, msg, src=None):
        half, stage, combo, kind = msg
        axis = axes_of(half)[::-1][stage]
        sign = 1 if kind in ("a0", "l0", "l1", "y") else -1
        i = self.index[msg]
        box = self.box(msg)
        return pltpu.make_async_remote_copy(
            src_ref=box if src is None else src,
            dst_ref=box,
            send_sem=self.send_sem.at[i],
            recv_sem=self.recv_sem.at[i],
            device_id=peer(self.me, toward(axis, sign)),
            device_id_type=MESH,
        )

    def add(self, dst, terms, count):
        value = terms[0][0:count].astype(F32)
        for term in terms[1:]:
            value = value + term[0:count].astype(F32)
        dst[0:count] = value.astype(dst.dtype)

    def step(self, item):
        _, what, key = item
        if what == "send":
            self.copy(key, self.source(key)).start()
            self.sent.append(key)
        elif what == "wait":
            self.copy(key).wait_recv()
        elif what == "relay":
            half, stage, combo, kind = key
            box = self.box(key)
            sub = int(kind[1])
            mine = self.mine(half, stage, combo, 1 if kind == "a0" else 3, sub)
            self.add(box, (mine, box), inner(half, sub).size)
        elif what == "pair":
            half, c = key
            box = self.pair.at[half, c]
            self.add(box, (self.three.at[half, self.group(0, (0, c)), 1], box), inner(half, None).size)
        else:
            half, stage, combo = key
            left = self.three.at[half, self.group(stage, combo), 1]
            right = self.three.at[half, self.group(stage, combo), 2]
            mine = self.mine(half, stage, combo, 0)
            dst = self.out.at[span(half, None)] if stage == 2 else left
            self.add(dst, (mine, left, right), inner(half, None).size)

    def finish(self):
        for key in self.sent:
            self.copy(key, self.source(key)).wait_send()


def back_kernel(classes, wt, spec, stat, out, logz, own, three, pair, tab, flat, seen, send_sem, recv_sem, stat_send, stat_recv):
    i = pl.program_id(0)
    me = place()
    x, y, z, cls = me
    work = Scatter(me, own, three, pair, out, send_sem, recv_sem)
    last = len(BLOCKS) - 1
    due = {}
    for item in work.steps:
        at = min(last, max(0, math.ceil(item[0] / BLOCK_UNITS - 0.001) - 1))
        due.setdefault(at, []).append(item)

    @pl.when(i == 0)
    def _():
        dp = slot(me, (0, 0, 0))
        barrier = pltpu.get_barrier_semaphore()
        there = [peer(me, toward(*move)) for move in ((0, 1), (0, -1), (1, 1), (2, 1), (2, -1))]
        others = [(dp, (cls + k) % 4) for k in (1, 2, 3)]
        for device in there + others:
            pl.semaphore_signal(barrier, inc=1, device_id=device, device_id_type=MESH)
        pl.semaphore_wait(barrier, len(there) + len(others))
        copies = []
        for k, device in enumerate(others):
            copy = pltpu.make_async_remote_copy(
                src_ref=stat,
                dst_ref=seen.at[k],
                send_sem=stat_send.at[k],
                recv_sem=stat_recv.at[k],
                device_id=device,
                device_id_type=MESH,
            )
            copy.start()
            copies.append(copy)
        for copy in copies:
            copy.wait()
        peaks = [stat[0]] + [seen[k, 0] for k in range(3)]
        masses = [stat[1]] + [seen[k, 1] for k in range(3)]
        top = jnp.maximum(jnp.maximum(peaks[0], peaks[1]), jnp.maximum(peaks[2], peaks[3]))
        mass = masses[0] * jnp.exp(peaks[0] - top)
        for k in range(1, 4):
            mass = mass + masses[k] * jnp.exp(peaks[k] - top)
        total = top + jnp.log(mass)
        logz[...] = total
        scale = jnp.concatenate([jnp.exp(peaks[0] - total)] * (QROWS // 8), 0)
        for g in range(FOLD):
            tab[g] = (spec[g] * scale).T.astype(BF16)

    dz = jnp.int32(0)
    dy = jnp.int32(0)
    for at, (bz, by) in enumerate(BLOCKS):
        dz = jnp.where(i == at, bz, dz)
        dy = jnp.where(i == at, by, dy)
    base = (((z + dz) % 4) * 2 + (y + dy) % 2) * 4
    for o in range(4):
        for j in range(9):
            g, sg = fold_of(o * 9 + j)
            both = jnp.dot(tab[g], wt[o * 9 + j], preferred_element_type=F32)
            a, b = both[:CPAD], both[CPAD:]
            rows = CPAD if j < 8 else HALF_ROWS - 8 * classes
            flat[o, 0, pl.ds(j * classes, rows), :] = (a[:, :128] - sg * b[:, 128:])[:rows]
            flat[o, 1, pl.ds(j * classes, rows), :] = (a[:, 128:] + sg * b[:, :128])[:rows]
        own[base + o] = flat[o].astype(BF16).reshape(TILES, 16, 128)

    for at in range(len(BLOCKS)):

        @pl.when(i == at)
        def _(at=at):
            for item in due.get(at, []):
                work.step(item)
            if at == last:
                work.finish()


def block_index(i):
    dp = lax.axis_index("dp")
    dz = jnp.int32(0)
    dy = jnp.int32(0)
    for at, (bz, by) in enumerate(BLOCKS):
        dz = jnp.where(i == at, bz, dz)
        dy = jnp.where(i == at, by, dy)
    return ((dp // 8 + dz) % 4) * 2 + ((dp // 4) % 2 + dy) % 2, 0, 0


def back(wt, spec, stat, classes):
    steps, index = scatter_keys()
    whole = pl.BlockSpec(memory_space=pltpu.VMEM)
    owners = SIZES[0] * SIZES[1] * SIZES[2]
    half = (TILES // 2 + 1, 16, 128)
    return pl.pallas_call(
        functools.partial(back_kernel, classes),
        grid=(len(BLOCKS),),
        out_shape=(jax.ShapeDtypeStruct((TILES, 16, 128), F32), jax.ShapeDtypeStruct((8, 128), F32)),
        in_specs=[pl.BlockSpec((ROTS, QROWS, 256), block_index), whole, whole],
        out_specs=(whole, whole),
        scratch_shapes=[
            pltpu.VMEM((owners, TILES, 16, 128), BF16),
            pltpu.VMEM((2, 9, 3) + half, BF16),
            pltpu.VMEM((2, 4) + half, BF16),
            pltpu.VMEM((FOLD, 128, QROWS), BF16),
            pltpu.VMEM((4, 2, HALF_ROWS, 128), F32),
            pltpu.VMEM((3, 2, 8, 128), F32),
            pltpu.SemaphoreType.DMA((len(index),)),
            pltpu.SemaphoreType.DMA((len(index),)),
            pltpu.SemaphoreType.DMA((3,)),
            pltpu.SemaphoreType.DMA((3,)),
        ],
        compiler_params=pltpu.CompilerParams(
            collective_id=2, has_side_effects=True, vmem_limit_bytes=48 * 2**20
        ),
        name="back",
    )(wt, spec, stat)


def twist_tables(freq, rot_offset):
    idx = (freq[:, None] * rot_offset[None, :]) % ANGLES
    rad = idx.astype(F32) * (2.0 * math.pi / ANGLES)
    return jnp.cos(rad)[:, :, None], jnp.sin(rad)[:, :, None]


def twist_refs(references, cos, sin):
    re = references[:, 0].astype(F32)
    im = references[:, 1].astype(F32)
    both = jnp.stack([re * cos + im * sin, im * cos - re * sin], 0).astype(BF16)
    both = both.reshape(2, -1, both.shape[3])
    both = jnp.pad(both, ((0, 0), (0, HALF_ROWS - both.shape[1]), (0, 0)))
    return both.reshape(TILES, 16, both.shape[2])


def untwist(sums, cos, sin, block, classes):
    rows = sums.reshape(2, HALF_ROWS, -1)[:, : block * classes].reshape(2, block, classes, -1)
    re, im = rows[0], rows[1]
    return jnp.stack([re * cos - im * sin, re * sin + im * cos], 1)


def order_angles(particles):
    return jnp.concatenate([particles[:, :, 0::2], particles[:, :, 1::2]], 2)


def local(particles, references, ctf_table, rot_offset, prior_shift, defocus_group):
    block, _, classes = references.shape[:3]
    freq = lax.axis_index("dp") * block + jnp.arange(block, dtype=jnp.int32)
    cos, sin = twist_tables(freq, rot_offset)
    wt, refs = transform(
        prior_shift, defocus_group, order_angles(particles), ctf_table, twist_refs(references, cos, sin)
    )
    spec, peak, mass, post = match(defocus_group, wt, refs, ctf_table, classes)
    sums, total = back(wt, spec, jnp.stack([peak, mass]), classes)
    posterior = post[:, :classes] * jnp.exp(peak[:, :classes] - total[:, :classes])
    return total[:, 0], posterior, untwist(sums, cos, sin, block, classes)


def solution(mesh):
    placed = (
        P("dp", None, None, None),
        P("dp", None, "cls", None),
        P(),
        P("cls"),
        P("dp", None),
        P("dp"),
    )
    return jax.shard_map(
        local,
        mesh=mesh,
        in_specs=placed,
        out_specs=(P("dp"), P("dp", "cls"), P("dp", None, "cls", None)),
        check_vma=False,
    )
```

```python
import functools
import heapq
import math

import jax
import jax.numpy as jnp
import numpy as np
from jax import lax
from jax.experimental import pallas as pl
from jax.experimental.pallas import tpu as pltpu
from jax.sharding import PartitionSpec as P

ROTS = 36
SIDE = 5
SHIFTS = SIDE * SIDE
ANGLES = 288
CYCLES = 128
HALF = ANGLES // 2
REACH = 10
FOLD = ROTS // 2 + 1
IPAD = 72
QROWS = 208
CPAD = 64
F32 = jnp.float32
BF16 = jnp.bfloat16
MESH = pl.DeviceIdType.MESH


def phase_tables():
    order = np.concatenate([np.arange(0, ANGLES, 2), np.arange(1, ANGLES, 2)])
    theta = 2.0 * np.pi * order / ANGLES
    radius = (np.arange(CYCLES) + 1) / (2.0 * CYCLES)
    count = np.arange(REACH + 1)
    out = []
    for wave in (np.cos(theta), np.sin(theta)):
        arg = 2.0 * np.pi * count[:, None, None] * wave[None, :, None] * radius[None, None, :]
        out.append(np.stack([np.cos(arg), np.sin(arg)], 1).astype(np.float32))
    return out


def dft_tables():
    row = np.arange(IPAD)
    out = []
    for start in (0, 1):
        t = np.arange(start, ANGLES, 2)
        ang = 2.0 * np.pi * ((row[:, None] * t[None, :]) % ANGLES) / ANGLES
        cos, sin = np.cos(ang), np.sin(ang)
        quarter = 2.0 * np.pi * ((IPAD * t) % ANGLES) / ANGLES
        sin[0] = np.rint(np.sin(quarter) if start else np.cos(quarter))
        out.append(np.concatenate([cos, sin], 0).astype(np.float32))
    return out


def rotation_coefs():
    k = np.arange(FOLD)
    ang = 2.0 * np.pi * ((k[:, None] * k[None, :]) % ROTS) / ROTS
    cos, sin = np.cos(ang), np.sin(ang)
    lanes = np.arange(128) < CPAD
    fwd = np.where(lanes, cos[:, :, None], -sin[:, :, None]) / ANGLES
    bwd = np.where(lanes, cos[:, :, None], sin[:, :, None])
    return fwd.astype(np.float32), bwd.astype(np.float32)


SIZES = (4, 2, 4)
TILES = 57
PARTS = ((0, 15, 29), (29, 43, 57))
LATE = 0.35


def place():
    dp = lax.axis_index("dp")
    return dp % 4, (dp // 4) % 2, dp // 8, lax.axis_index("cls")


def peer(me, rel):
    x, y, z, cls = me
    return ((((z + rel[2]) % 4) * 2 + (y + rel[1]) % 2) * 4 + (x + rel[0]) % 4, cls)


def slot(me, rel):
    return peer(me, rel)[0]


def toward(axis, sign):
    move = [0, 0, 0]
    move[axis] = sign
    return tuple(move)


def greet(me):
    barrier = pltpu.get_barrier_semaphore()
    moves = [toward(0, 1), toward(0, -1), toward(1, 1), toward(2, 1), toward(2, -1)]
    for move in moves:
        pl.semaphore_signal(barrier, inc=1, device_id=peer(me, move), device_id_type=MESH)
    pl.semaphore_wait(barrier, len(moves))


def axes_of(half):
    return (0, 1, 2) if half == 0 else (2, 1, 0)


def span(half, sub):
    low, mid, high = PARTS[half]
    first, end = ((low, high), (low, mid), (mid, high))[0 if sub is None else sub + 1]
    return pl.ds(first, end - first)


def share(half, sub):
    low, mid, high = PARTS[half]
    return ((high - low) if sub is None else (mid - low, high - mid)[sub]) * 2.0 / TILES


class Links:
    def __init__(self):
        self.free, self.heap, self.count = {}, [], 0

    def send(self, t, axis, sign, size, key):
        start = max(t, self.free.get((axis, sign), 0.0))
        self.free[(axis, sign)] = start + size
        self.push(start + size + LATE, key)

    def push(self, t, key):
        self.count += 1
        heapq.heappush(self.heap, (t, self.count, key))

    def pop(self):
        t, _, key = heapq.heappop(self.heap)
        return t, key


def gather_plan():
    links, plan, got = Links(), [], {}
    for half in (0, 1):
        links.push(0.0, (half, (0, 0, 0), None))
    while links.heap:
        t, key = links.pop()
        half, rel, sub = key
        order = axes_of(half)
        sends = []

        def go(axis, sign, sub):
            seen = list(rel)
            seen[axis] = (seen[axis] - sign) % SIZES[axis]
            there = (half, tuple(seen), sub)
            sends.append((half, rel, sub, axis, sign, there))
            links.send(t, axis, sign, share(half, sub), there)

        got[half, rel] = got.get((half, rel), 0) + 1
        if sub is None or got[half, rel] == 2:
            last = max([i for i in range(3) if rel[order[i]]], default=-1)
            for i in range(2, last, -1):
                if order[i] == 1:
                    go(1, 1, None)
                else:
                    go(order[i], 1, None)
                    go(order[i], -1, None)
            if last >= 0 and order[last] != 1:
                if rel[order[last]] == 3:
                    go(order[last], 1, 0)
                elif rel[order[last]] == 1:
                    go(order[last], -1, 1)
        plan.append((t, None if rel == (0, 0, 0) else key, sends))
    return plan


def gather_keys():
    plan = gather_plan()
    recv = {step[1]: i for i, step in enumerate(s for s in plan if s[1] is not None)}
    return plan, recv


class Gather:
    def __init__(self, me, own, store, send_sem, recv_sem):
        self.me, self.own, self.store = me, own, store
        self.send_sem, self.recv_sem = send_sem, recv_sem
        self.plan, self.recv = gather_keys()
        self.sent = []

    def copy(self, index, half, rel, sub, axis, sign, there):
        where = span(half, sub)
        here = self.own.at[where] if rel == (0, 0, 0) else self.store.at[slot(self.me, rel), where]
        return pltpu.make_async_remote_copy(
            src_ref=here,
            dst_ref=self.store.at[slot(self.me, rel), where],
            send_sem=self.send_sem.at[index],
            recv_sem=self.recv_sem.at[self.recv[there]],
            device_id=peer(self.me, toward(axis, sign)),
            device_id_type=MESH,
        )

    def arrived(self, key):
        half, rel, sub = key
        here = self.store.at[slot(self.me, rel), span(half, sub)]
        pltpu.make_async_remote_copy(
            src_ref=here,
            dst_ref=here,
            send_sem=self.send_sem.at[0],
            recv_sem=self.recv_sem.at[self.recv[key]],
            device_id=peer(self.me, (1, 0, 0)),
            device_id_type=MESH,
        ).wait_recv()

    def step(self, item):
        _, key, sends = item
        if key is not None:
            self.arrived(key)
        for send in sends:
            self.copy(len(self.sent), *send).start()
            self.sent.append(send)

    def finish(self):
        for index, send in enumerate(self.sent):
            self.copy(index, *send).wait_send()


GROUP = 8
STEPS = 26
PITCH = 4 * IPAD + 3
UNIT_STEPS = 1.6


def transform_kernel(shift, group, part, ctf, txh, tyh, te, to, own, out, store, tx, ty, z1, xs, fr, fi, send_sem, recv_sem, own_sem, tab_sem):
    u = pl.program_id(0)
    me = place()
    work = Gather(me, own, store, send_sem, recv_sem)
    keep = pltpu.make_async_copy(own, store.at[slot(me, (0, 0, 0))], own_sem)
    due = {}
    for item in work.plan:
        at = 0 if item[1] is None else min(STEPS - 1, math.ceil(item[0] * UNIT_STEPS))
        due.setdefault(at, []).append(item)

    loads = [pltpu.make_async_copy(txh, tx, tab_sem.at[0]), pltpu.make_async_copy(tyh, ty, tab_sem.at[1])]

    @pl.when(u == 0)
    def _():
        for load in loads:
            load.start()
        greet(me)
        keep.start()

    for at in sorted(due):
        if at < STEPS - 1:

            @pl.when(u == at)
            def _(at=at):
                for item in due[at]:
                    work.step(item)

    @pl.when(u == 0)
    def _():
        for load in loads:
            load.wait()

    s = jnp.minimum(u, SHIFTS - 1)
    a = s // SIDE
    b = s % SIDE

    @pl.when((b == 0) & (u < SHIFTS))
    def _():
        def ramp(p, carry):
            sx = shift[p, 0] + a - SIDE // 2
            n = jnp.abs(sx)
            sg = jnp.where(sx < 0, -1.0, 1.0).astype(F32)
            for c in range(0, ANGLES, 48):
                rows = pl.ds(c, 48)
                re = part[p, 0, rows, :].astype(F32)
                im = part[p, 1, rows, :].astype(F32)
                co = tx[n, 0, rows, :]
                si = tx[n, 1, rows, :] * sg
                z1[p, 0, rows, :] = re * co + im * si
                z1[p, 1, rows, :] = im * co - re * si
            return carry

        lax.fori_loop(0, GROUP, ramp, 0)

    @pl.when(u < SHIFTS)
    def _():
        for p in range(GROUP):
            sy = shift[p, 1] + b - SIDE // 2
            n = jnp.abs(sy)
            sg = jnp.where(sy < 0, -1.0, 1.0).astype(F32)
            for c in range(0, ANGLES, 16):
                rows = pl.ds(c, 16)
                re = z1[p, 0, rows, :]
                im = z1[p, 1, rows, :]
                co = ty[n, 0, rows, :]
                si = ty[n, 1, rows, :] * sg
                xs[rows, 256 * p : 256 * p + 128] = (re * co + im * si).astype(BF16)
                xs[rows, 256 * p + 128 : 256 * p + 256] = (im * co - re * si).astype(BF16)
        even = jnp.dot(te[...], xs[0:HALF, :], preferred_element_type=F32)
        odd = jnp.dot(to[...], xs[HALF:, :], preferred_element_type=F32)
        for p in range(GROUP):
            j = (u % 2) * GROUP + p
            gain = ctf[pl.ds(group[p], 1), :]
            lo, hi = slice(256 * p, 256 * p + 128), slice(256 * p + 128, 256 * p + 256)
            for c in range(0, IPAD, 8):
                cos, sin = slice(c, c + 8), slice(IPAD + c, IPAD + c + 8)
                er, ei, fr_, fi_ = even[cos, lo], even[cos, hi], even[sin, lo], even[sin, hi]
                gr, gi, hr, hi_ = odd[cos, lo], odd[cos, hi], odd[sin, lo], odd[sin, hi]
                if c == 0:
                    for at, re, im in (
                        (0, fr_[0:1] + hi_[0:1], fi_[0:1] - hr[0:1]),
                        (1, fr_[0:1] - hi_[0:1], fi_[0:1] + hr[0:1]),
                    ):
                        fr[pl.ds(j * PITCH + 4 * IPAD + at, 1), :] = re * gain
                        fi[pl.ds(j * PITCH + 4 * IPAD + at, 1), :] = im * gain
                    rest = lax.broadcasted_iota(jnp.int32, (8, 128), 0) > 0
                    fr_, fi_, hr, hi_ = [jnp.where(rest, v, 0.0) for v in (fr_, fi_, hr, hi_)]
                u1 = (er + fi_) * gain
                u2 = (er - fi_) * gain
                w1 = (ei - fr_) * gain
                w2 = (ei + fr_) * gain
                v1 = (gr + hi_) * gain
                v2 = (gr - hi_) * gain
                y1 = (gi - hr) * gain
                y2 = (gi + hr) * gain
                for blk, (re, im) in enumerate(
                    ((u1 + v1, w1 + y1), (u1 - v1, w1 - y1), (u2 - v2, w2 - y2), (u2 + v2, w2 + y2))
                ):
                    rows = pl.ds(j * PITCH + blk * IPAD + c, 8)
                    fr[rows, :] = re
                    fi[rows, :] = im

    def emit(i, blk, m):
        rows = pl.ds(blk * IPAD + i, 2 * GROUP, stride=PITCH)
        out[m, :, 0:128] = fr[rows, :].astype(BF16)
        out[m, :, 128:256] = fi[rows, :].astype(BF16)

    @pl.when(u % 2 == 1)
    def _():
        def pack(i, carry):
            emit(i, 0, i)
            emit(i, 1, HALF + i)
            emit(i, 2, HALF - i)
            emit(i, 3, ANGLES - i)
            return carry

        emit(0, 0, 0)
        emit(0, 1, HALF)
        emit(0, 4, IPAD)
        emit(1, 4, HALF + IPAD)
        lax.fori_loop(1, HALF // 2, pack, 0, unroll=8)

    @pl.when(u == STEPS - 1)
    def _():
        for item in due.get(STEPS - 1, []):
            work.step(item)
        keep.wait()
        work.finish()


def transform(shift, group, part, ctf, own):
    tx, ty = phase_tables()
    te, to = dft_tables()
    plan, recv = gather_keys()
    whole = pl.BlockSpec(memory_space=pltpu.VMEM)
    near = pl.BlockSpec(memory_space=pltpu.SMEM)
    far = pl.BlockSpec(memory_space=pl.ANY)
    owners = SIZES[0] * SIZES[1] * SIZES[2]
    return pl.pallas_call(
        transform_kernel,
        grid=(STEPS,),
        out_shape=(
            jax.ShapeDtypeStruct((ANGLES, QROWS, 256), BF16),
            jax.ShapeDtypeStruct((owners,) + own.shape, own.dtype),
        ),
        in_specs=[near, near, whole, whole, far, far, whole, whole, whole],
        out_specs=(
            pl.BlockSpec((ANGLES, 2 * GROUP, 256), lambda u: (0, u // 2, 0)),
            pl.BlockSpec(memory_space=pl.ANY),
        ),
        scratch_shapes=[
            pltpu.VMEM((REACH + 1, 2, ANGLES, 128), F32),
            pltpu.VMEM((REACH + 1, 2, ANGLES, 128), F32),
            pltpu.VMEM((GROUP, 2, ANGLES, 128), F32),
            pltpu.VMEM((ANGLES, 256 * GROUP), BF16),
            pltpu.VMEM((2 * GROUP * PITCH + 8, 128), F32),
            pltpu.VMEM((2 * GROUP * PITCH + 8, 128), F32),
            pltpu.SemaphoreType.DMA((sum(len(s[2]) for s in plan),)),
            pltpu.SemaphoreType.DMA((len(recv),)),
            pltpu.SemaphoreType.DMA,
            pltpu.SemaphoreType.DMA((2,)),
        ],
        compiler_params=pltpu.CompilerParams(
            collective_id=1, has_side_effects=True, vmem_limit_bytes=56 * 2**20
        ),
        name="transform",
    )(shift, group, part, ctf, jnp.asarray(tx), jnp.asarray(ty), jnp.asarray(te, BF16), jnp.asarray(to, BF16), own)


H = FOLD // 2
HALF_ROWS = TILES * 8

def fold_of(r):
    return (r, 1) if r <= ROTS // 2 else (ROTS - r, -1)

def half_sums(parts, tab, k):
    even = parts[0] * tab[k, 0:1, :]
    for g in range(2, FOLD, 2):
        even = even + parts[g] * tab[k, g : g + 1, :]
    odd = parts[1] * tab[k, 1:2, :]
    for g in range(3, FOLD, 2):
        odd = odd + parts[g] * tab[k, g : g + 1, :]
    return even, odd

def match_kernel(classes, group, wt, refs, ctf, fwd, bwd, spec, peak, mass, post, acc, power, flat):
    d = pl.program_id(0)
    first = d == 0
    for o in range(4):
        flat[o, 0 : TILES * 16] = refs[o].reshape(TILES * 16, 128).astype(F32)

    def image(r, part):
        at = part * HALF_ROWS + (r % 9) * classes
        return flat[r // 9, pl.ds(at, CPAD), :]

    def product(r, squares):
        re, im = image(r, 0), image(r, 1)
        squares.append(re * re + im * im)
        re, im = re.astype(BF16), im.astype(BF16)
        if fold_of(r)[1] > 0:
            table = jnp.concatenate([jnp.concatenate([re, im], 1), jnp.concatenate([-im, re], 1)], 0)
        else:
            table = jnp.concatenate([jnp.concatenate([re, im], 1), jnp.concatenate([im, -re], 1)], 0)
        return lax.dot_general(wt[r], table, (((1,), (1,)), ((), ())), preferred_element_type=F32)

    @pl.when(first)
    def _():
        acc[...] = jnp.zeros_like(acc)
        power[...] = jnp.zeros_like(power)
        flat[:, TILES * 16 :] = jnp.zeros((4, 8, 128), F32)

    pw = power[...]
    for g in range(FOLD):
        squares = []
        y = product(g, squares)
        if 0 < g < FOLD - 1:
            y = y + product(ROTS - g, squares)
        acc[g] += y
        for term in squares:
            pw = pw + term
    power[...] = pw

    @pl.when(d == pl.num_programs(0) - 1)
    def _():
        gain = jnp.concatenate([ctf[pl.ds(group[p], 1), :] for p in range(8)], 0)
        half = lax.dot_general(
            gain * gain,
            power[...],
            (((1,), (1,)), ((), ())),
            precision=lax.Precision.HIGHEST,
            preferred_element_type=F32,
        ) * (0.5 / ANGLES)
        bias = jnp.concatenate([half, half], 1)
        lane = lax.broadcasted_iota(jnp.int32, (8, 128), 1)
        live = lane % CPAD < classes
        edge = lane < classes
        sign = jnp.where(lane < CPAD, 1.0, -1.0).astype(F32)
        low = -1e30

        def score(s, top):
            rows = pl.ds(pl.multiple_of(s * 8, 8), 8)
            parts = [acc[g, rows, :] for g in range(FOLD)]
            for k in range(H + 1):
                even, odd = half_sums(parts, fwd, k)
                y, w = even + odd, even - odd
                both = [(k, y * sign + pltpu.roll(y, CPAD, 1))]
                if k < H:
                    both.append((FOLD - 1 - k, w + pltpu.roll(w * sign, CPAD, 1)))
                for at, z in both:
                    z = z - bias
                    z = jnp.where(edge if at in (0, FOLD - 1) else live, z, low)
                    spec[at, rows, :] = z
                    top = jnp.maximum(top, z)
            return top

        top = lax.fori_loop(0, SHIFTS, score, jnp.full((8, 128), low, F32), unroll=5)
        top = jnp.max(top, axis=1, keepdims=True)

        def weigh(s, total):
            rows = pl.ds(pl.multiple_of(s * 8, 8), 8)
            parts = []
            for k in range(FOLD):
                e = jnp.exp(spec[k, rows, :] - top)
                total = total + e
                parts.append(e * sign + pltpu.roll(e, CPAD, 1))
            for g in range(H + 1):
                even, odd = half_sums(parts, bwd, g)
                spec[g, rows, :] = even + odd
                if g < H:
                    spec[FOLD - 1 - g, rows, :] = (even - odd) * sign
            return total

        total = lax.fori_loop(0, SHIFTS, weigh, jnp.zeros((8, 128), F32), unroll=5)
        spec[:, SHIFTS * 8 :, :] = jnp.zeros((FOLD, QROWS - SHIFTS * 8, 128), F32)
        peak[...] = jnp.broadcast_to(top, (8, 128))
        mass[...] = jnp.broadcast_to(jnp.sum(total, axis=1, keepdims=True), (8, 128))
        post[...] = total + pltpu.roll(total, CPAD, 1)

def match(group, wt, refs, ctf, classes):
    fwd, bwd = rotation_coefs()
    small = jax.ShapeDtypeStruct((8, 128), F32)
    whole = pl.BlockSpec(memory_space=pltpu.VMEM)
    return pl.pallas_call(
        functools.partial(match_kernel, classes),
        grid=(ANGLES // ROTS,),
        out_shape=(jax.ShapeDtypeStruct((FOLD, QROWS, 128), F32), small, small, small),
        in_specs=[pl.BlockSpec(memory_space=pltpu.SMEM), pl.BlockSpec((ROTS, QROWS, 256), lambda d: (d, 0, 0)),
                  pl.BlockSpec((4, TILES, 16, 128), lambda d: (d, 0, 0, 0)), whole, whole, whole],
        out_specs=(whole,) * 4,
        scratch_shapes=[pltpu.VMEM((FOLD, QROWS, 128), F32), pltpu.VMEM((CPAD, 128), F32), pltpu.VMEM((4, TILES * 16 + 8, 128), F32)],
        compiler_params=pltpu.CompilerParams(vmem_limit_bytes=48 * 2**20),
        name="match",
    )(group, wt, refs, ctf, jnp.asarray(fwd), jnp.asarray(bwd))

COMBOS = [(ry, c) for ry in (1, 0) for c in (2, 1, 3, 0)]
BLOCKS = [(2, 1), (2, 0), (1, 1), (3, 1), (1, 0), (3, 0), (0, 1), (0, 0)]
BLOCK_UNITS = 0.9


def scatter_plan():
    links, steps, got, done = Links(), [], set(), set()

    def send(t, half, stage, combo, kind):
        axis = axes_of(half)[::-1][stage]
        sign = 1 if kind in ("a0", "l0", "l1", "y") else -1
        size = share(half, None if kind == "y" else int(kind[1]))
        msg = (half, stage, combo, kind)
        steps.append((t, "send", msg))
        links.send(t, axis, sign, size, msg)

    def have(half, stage, combo, k):
        if stage == 2:
            return (half, 2, k) in done
        return ((k, combo[0]) if half == 0 else (combo[1], combo[0])) in done

    def ready(t, half, stage, combo, k):
        if k == 2:
            send(t, half, stage, combo, "a0")
            send(t, half, stage, combo, "a1")
        elif k == 1:
            send(t, half, stage, combo, "l1")
            relay(t, half, stage, combo, "a0")
        elif k == 3:
            send(t, half, stage, combo, "r0")
            relay(t, half, stage, combo, "a1")
        else:
            total(t, half, stage, combo)

    def relay(t, half, stage, combo, kind):
        k = 1 if kind == "a0" else 3
        if (half, stage, combo, kind) in got and have(half, stage, combo, k):
            steps.append((t, "relay", (half, stage, combo, kind)))
            send(t, half, stage, combo, "l0" if kind == "a0" else "r1")

    def total(t, half, stage, combo):
        kinds = ("l0", "l1", "r0", "r1")
        if all((half, stage, combo, kind) in got for kind in kinds) and have(half, stage, combo, 0):
            steps.append((t, "total", (half, stage, combo)))
            if stage == 0:
                done.add((half, 0, combo, "s"))
                if combo[0] == 1:
                    send(t, half, 1, combo[1], "y")
                else:
                    second(t, half, combo[1])

    def second(t, half, c):
        if (half, 0, (0, c), "s") in done and (half, 1, c, "y") in got:
            steps.append((t, "pair", (half, c)))
            done.add((half, 2, c))
            ready(t, half, 2, None, c)

    for i, block in enumerate(BLOCKS):
        links.push((i + 1) * BLOCK_UNITS, ("block", block))
    while links.heap:
        t, key = links.pop()
        if key[0] == "block":
            z, y = key[1]
            done.add((z, y))
            for x in (2, 1, 3, 0):
                ready(t, 0, 0, (y, x), z)
                ready(t, 1, 0, (y, z), x)
            continue
        half, stage, combo, kind = key
        steps.append((t, "wait", key))
        got.add(key)
        if kind == "y":
            second(t, half, combo)
        elif kind in ("a0", "a1"):
            relay(t, half, stage, combo, kind)
        else:
            total(t, half, stage, combo)
    return steps


def scatter_keys():
    steps = scatter_plan()
    return steps, {s[2]: i for i, s in enumerate(s for s in steps if s[1] == "send")}


def inner(half, sub):
    low, mid, high = PARTS[half]
    first, end = ((low, high), (low, mid), (mid, high))[0 if sub is None else sub + 1]
    return pl.ds(first - low, end - first)


class Scatter:
    def __init__(self, me, own, three, pair, out, send_sem, recv_sem):
        self.me, self.own, self.three, self.pair, self.out = me, own, three, pair, out
        self.send_sem, self.recv_sem = send_sem, recv_sem
        self.steps, self.index = scatter_keys()
        self.sent = []

    def group(self, stage, combo):
        return 8 if stage == 2 else COMBOS.index(combo)

    def mine(self, half, stage, combo, k, sub=None):
        if stage == 2:
            return self.pair.at[half, k, inner(half, sub)]
        order = axes_of(half)[::-1]
        rel = [0, 0, 0]
        rel[order[0]] = k
        rel[1] = combo[0]
        rel[order[2]] = combo[1]
        return self.own.at[slot(self.me, rel), span(half, sub)]

    def box(self, msg):
        half, stage, combo, kind = msg
        if kind == "y":
            return self.pair.at[half, combo, inner(half, None)]
        which = {"a": 0, "l": 1, "r": 2}[kind[0]]
        return self.three.at[half, self.group(stage, combo), which, inner(half, int(kind[1]))]

    def source(self, msg):
        half, stage, combo, kind = msg
        if kind == "y":
            return self.three.at[half, self.group(0, (1, combo)), 1, inner(half, None)]
        sub = int(kind[1])
        if kind in ("a0", "a1"):
            return self.mine(half, stage, combo, 2, sub)
        if kind == "l1":
            return self.mine(half, stage, combo, 1, sub)
        if kind == "r0":
            return self.mine(half, stage, combo, 3, sub)
        return self.three.at[half, self.group(stage, combo), 0, inner(half, sub)]

    def copy(self, msg, src=None):
        half, stage, combo, kind = msg
        axis = axes_of(half)[::-1][stage]
        sign = 1 if kind in ("a0", "l0", "l1", "y") else -1
        i = self.index[msg]
        box = self.box(msg)
        return pltpu.make_async_remote_copy(
            src_ref=box if src is None else src,
            dst_ref=box,
            send_sem=self.send_sem.at[i],
            recv_sem=self.recv_sem.at[i],
            device_id=peer(self.me, toward(axis, sign)),
            device_id_type=MESH,
        )

    def add(self, dst, terms, count):
        value = terms[0][0:count].astype(F32)
        for term in terms[1:]:
            value = value + term[0:count].astype(F32)
        dst[0:count] = value.astype(dst.dtype)

    def step(self, item):
        _, what, key = item
        if what == "send":
            self.copy(key, self.source(key)).start()
            self.sent.append(key)
        elif what == "wait":
            self.copy(key).wait_recv()
        elif what == "relay":
            half, stage, combo, kind = key
            box = self.box(key)
            sub = int(kind[1])
            mine = self.mine(half, stage, combo, 1 if kind == "a0" else 3, sub)
            self.add(box, (mine, box), inner(half, sub).size)
        elif what == "pair":
            half, c = key
            box = self.pair.at[half, c]
            self.add(box, (self.three.at[half, self.group(0, (0, c)), 1], box), inner(half, None).size)
        else:
            half, stage, combo = key
            left = self.three.at[half, self.group(stage, combo), 1]
            right = self.three.at[half, self.group(stage, combo), 2]
            mine = self.mine(half, stage, combo, 0)
            dst = self.out.at[span(half, None)] if stage == 2 else left
            self.add(dst, (mine, left, right), inner(half, None).size)

    def finish(self):
        for key in self.sent:
            self.copy(key, self.source(key)).wait_send()


def back_kernel(classes, wt, spec, stat, out, logz, own, three, pair, tab, flat, seen, send_sem, recv_sem, stat_send, stat_recv):
    i = pl.program_id(0)
    me = place()
    x, y, z, cls = me
    work = Scatter(me, own, three, pair, out, send_sem, recv_sem)
    last = len(BLOCKS) - 1
    due = {}
    for item in work.steps:
        at = min(last, max(0, math.ceil(item[0] / BLOCK_UNITS - 0.001) - 1))
        due.setdefault(at, []).append(item)

    @pl.when(i == 0)
    def _():
        dp = slot(me, (0, 0, 0))
        barrier = pltpu.get_barrier_semaphore()
        there = [peer(me, toward(*move)) for move in ((0, 1), (0, -1), (1, 1), (2, 1), (2, -1))]
        others = [(dp, (cls + k) % 4) for k in (1, 2, 3)]
        for device in there + others:
            pl.semaphore_signal(barrier, inc=1, device_id=device, device_id_type=MESH)
        pl.semaphore_wait(barrier, len(there) + len(others))
        copies = []
        for k, device in enumerate(others):
            copy = pltpu.make_async_remote_copy(
                src_ref=stat,
                dst_ref=seen.at[k],
                send_sem=stat_send.at[k],
                recv_sem=stat_recv.at[k],
                device_id=device,
                device_id_type=MESH,
            )
            copy.start()
            copies.append(copy)
        for copy in copies:
            copy.wait()
        peaks = [stat[0]] + [seen[k, 0] for k in range(3)]
        masses = [stat[1]] + [seen[k, 1] for k in range(3)]
        top = jnp.maximum(jnp.maximum(peaks[0], peaks[1]), jnp.maximum(peaks[2], peaks[3]))
        mass = masses[0] * jnp.exp(peaks[0] - top)
        for k in range(1, 4):
            mass = mass + masses[k] * jnp.exp(peaks[k] - top)
        total = top + jnp.log(mass)
        logz[...] = total
        scale = jnp.concatenate([jnp.exp(peaks[0] - total)] * (QROWS // 8), 0)
        for g in range(FOLD):
            tab[g] = (spec[g] * scale).T.astype(BF16)

    dz = jnp.int32(0)
    dy = jnp.int32(0)
    for at, (bz, by) in enumerate(BLOCKS):
        dz = jnp.where(i == at, bz, dz)
        dy = jnp.where(i == at, by, dy)
    base = (((z + dz) % 4) * 2 + (y + dy) % 2) * 4
    for o in range(4):
        for j in range(9):
            g, sg = fold_of(o * 9 + j)
            both = jnp.dot(tab[g], wt[o * 9 + j], preferred_element_type=F32)
            a, b = both[:CPAD], both[CPAD:]
            rows = CPAD if j < 8 else HALF_ROWS - 8 * classes
            flat[o, 0, pl.ds(j * classes, rows), :] = (a[:, :128] - sg * b[:, 128:])[:rows]
            flat[o, 1, pl.ds(j * classes, rows), :] = (a[:, 128:] + sg * b[:, :128])[:rows]
        own[base + o] = flat[o].astype(BF16).reshape(TILES, 16, 128)

    for at in range(len(BLOCKS)):

        @pl.when(i == at)
        def _(at=at):
            for item in due.get(at, []):
                work.step(item)
            if at == last:
                work.finish()


def block_index(i):
    dp = lax.axis_index("dp")
    dz = jnp.int32(0)
    dy = jnp.int32(0)
    for at, (bz, by) in enumerate(BLOCKS):
        dz = jnp.where(i == at, bz, dz)
        dy = jnp.where(i == at, by, dy)
    return ((dp // 8 + dz) % 4) * 2 + ((dp // 4) % 2 + dy) % 2, 0, 0


def back(wt, spec, stat, classes):
    steps, index = scatter_keys()
    whole = pl.BlockSpec(memory_space=pltpu.VMEM)
    owners = SIZES[0] * SIZES[1] * SIZES[2]
    half = (TILES // 2 + 1, 16, 128)
    return pl.pallas_call(
        functools.partial(back_kernel, classes),
        grid=(len(BLOCKS),),
        out_shape=(jax.ShapeDtypeStruct((TILES, 16, 128), F32), jax.ShapeDtypeStruct((8, 128), F32)),
        in_specs=[pl.BlockSpec((ROTS, QROWS, 256), block_index), whole, whole],
        out_specs=(whole, whole),
        scratch_shapes=[
            pltpu.VMEM((owners, TILES, 16, 128), BF16),
            pltpu.VMEM((2, 9, 3) + half, BF16),
            pltpu.VMEM((2, 4) + half, BF16),
            pltpu.VMEM((FOLD, 128, QROWS), BF16),
            pltpu.VMEM((4, 2, HALF_ROWS, 128), F32),
            pltpu.VMEM((3, 2, 8, 128), F32),
            pltpu.SemaphoreType.DMA((len(index),)),
            pltpu.SemaphoreType.DMA((len(index),)),
            pltpu.SemaphoreType.DMA((3,)),
            pltpu.SemaphoreType.DMA((3,)),
        ],
        compiler_params=pltpu.CompilerParams(
            collective_id=2, has_side_effects=True, vmem_limit_bytes=48 * 2**20
        ),
        name="back",
    )(wt, spec, stat)


def twist_tables(freq, rot_offset):
    idx = (freq[:, None] * rot_offset[None, :]) % ANGLES
    rad = idx.astype(F32) * (2.0 * math.pi / ANGLES)
    return jnp.cos(rad)[:, :, None], jnp.sin(rad)[:, :, None]


def twist_refs(references, cos, sin):
    re = references[:, 0].astype(F32)
    im = references[:, 1].astype(F32)
    both = jnp.stack([re * cos + im * sin, im * cos - re * sin], 0).astype(BF16)
    both = both.reshape(2, -1, both.shape[3])
    both = jnp.pad(both, ((0, 0), (0, HALF_ROWS - both.shape[1]), (0, 0)))
    return both.reshape(TILES, 16, both.shape[2])


def untwist(sums, cos, sin, block, classes):
    rows = sums.reshape(2, HALF_ROWS, -1)[:, : block * classes].reshape(2, block, classes, -1)
    re, im = rows[0], rows[1]
    return jnp.stack([re * cos - im * sin, re * sin + im * cos], 1)


def order_angles(particles):
    return jnp.concatenate([particles[:, :, 0::2], particles[:, :, 1::2]], 2)


def local(particles, references, ctf_table, rot_offset, prior_shift, defocus_group):
    block, _, classes = references.shape[:3]
    freq = lax.axis_index("dp") * block + jnp.arange(block, dtype=jnp.int32)
    cos, sin = twist_tables(freq, rot_offset)
    wt, refs = transform(
        prior_shift, defocus_group, order_angles(particles), ctf_table, twist_refs(references, cos, sin)
    )
    spec, peak, mass, post = match(defocus_group, wt, refs, ctf_table, classes)
    sums, total = back(wt, spec, jnp.stack([peak, mass]), classes)
    posterior = post[:, :classes] * jnp.exp(peak[:, :classes] - total[:, :classes])
    return total[:, 0], posterior, untwist(sums, cos, sin, block, classes)


def solution(mesh):
    placed = (
        P("dp", None, None, None),
        P("dp", None, "cls", None),
        P(),
        P("cls"),
        P("dp", None),
        P("dp"),
    )
    return jax.shard_map(
        local,
        mesh=mesh,
        in_specs=placed,
        out_specs=(P("dp"), P("dp", "cls"), P("dp", None, "cls", None)),
        check_vma=False,
    )
```

```python
import functools
import heapq
import math

import jax
import jax.numpy as jnp
import numpy as np
from jax import lax
from jax.experimental import pallas as pl
from jax.experimental.pallas import tpu as pltpu
from jax.sharding import PartitionSpec as P

ROTS = 36
SIDE = 5
SHIFTS = SIDE * SIDE
ANGLES = 288
CYCLES = 128
HALF = ANGLES // 2
REACH = 10
FOLD = ROTS // 2 + 1
IPAD = 72
QROWS = 208
CPAD = 64
F32 = jnp.float32
BF16 = jnp.bfloat16
MESH = pl.DeviceIdType.MESH


def phase_tables():
    order = np.concatenate([np.arange(0, ANGLES, 2), np.arange(1, ANGLES, 2)])
    theta = 2.0 * np.pi * order / ANGLES
    radius = (np.arange(CYCLES) + 1) / (2.0 * CYCLES)
    count = np.arange(REACH + 1)
    out = []
    for wave in (np.cos(theta), np.sin(theta)):
        arg = 2.0 * np.pi * count[:, None, None] * wave[None, :, None] * radius[None, None, :]
        out.append(np.stack([np.cos(arg), np.sin(arg)], 1).astype(np.float32))
    return out


def dft_tables():
    row = np.arange(IPAD)
    out = []
    for start in (0, 1):
        t = np.arange(start, ANGLES, 2)
        ang = 2.0 * np.pi * ((row[:, None] * t[None, :]) % ANGLES) / ANGLES
        cos, sin = np.cos(ang), np.sin(ang)
        quarter = 2.0 * np.pi * ((IPAD * t) % ANGLES) / ANGLES
        sin[0] = np.rint(np.sin(quarter) if start else np.cos(quarter))
        out.append(np.concatenate([cos, sin], 0).astype(np.float32))
    return out


def rotation_coefs():
    k = np.arange(FOLD)
    ang = 2.0 * np.pi * ((k[:, None] * k[None, :]) % ROTS) / ROTS
    cos, sin = np.cos(ang), np.sin(ang)
    lanes = np.arange(128) < CPAD
    fwd = np.where(lanes, cos[:, :, None], -sin[:, :, None]) / ANGLES
    bwd = np.where(lanes, cos[:, :, None], sin[:, :, None])
    return fwd.astype(np.float32), bwd.astype(np.float32)


SIZES = (4, 2, 4)
TILES = 57
PARTS = ((0, 15, 29), (29, 43, 57))
LATE = 0.35


def place():
    dp = lax.axis_index("dp")
    return dp % 4, (dp // 4) % 2, dp // 8, lax.axis_index("cls")


def peer(me, rel):
    x, y, z, cls = me
    return ((((z + rel[2]) % 4) * 2 + (y + rel[1]) % 2) * 4 + (x + rel[0]) % 4, cls)


def slot(me, rel):
    return peer(me, rel)[0]


def toward(axis, sign):
    move = [0, 0, 0]
    move[axis] = sign
    return tuple(move)


def greet(me):
    barrier = pltpu.get_barrier_semaphore()
    moves = [toward(0, 1), toward(0, -1), toward(1, 1), toward(2, 1), toward(2, -1)]
    for move in moves:
        pl.semaphore_signal(barrier, inc=1, device_id=peer(me, move), device_id_type=MESH)
    pl.semaphore_wait(barrier, len(moves))


def axes_of(half):
    return (0, 1, 2) if half == 0 else (2, 1, 0)


def span(half, sub):
    low, mid, high = PARTS[half]
    first, end = ((low, high), (low, mid), (mid, high))[0 if sub is None else sub + 1]
    return pl.ds(first, end - first)


def share(half, sub):
    low, mid, high = PARTS[half]
    return ((high - low) if sub is None else (mid - low, high - mid)[sub]) * 2.0 / TILES


class Links:
    def __init__(self):
        self.free, self.heap, self.count = {}, [], 0

    def send(self, t, axis, sign, size, key):
        start = max(t, self.free.get((axis, sign), 0.0))
        self.free[(axis, sign)] = start + size
        self.push(start + size + LATE, key)

    def push(self, t, key):
        self.count += 1
        heapq.heappush(self.heap, (t, self.count, key))

    def pop(self):
        t, _, key = heapq.heappop(self.heap)
        return t, key


def gather_plan():
    links, plan, got = Links(), [], {}
    for half in (0, 1):
        links.push(0.0, (half, (0, 0, 0), None))
    while links.heap:
        t, key = links.pop()
        half, rel, sub = key
        order = axes_of(half)
        sends = []

        def go(axis, sign, sub):
            seen = list(rel)
            seen[axis] = (seen[axis] - sign) % SIZES[axis]
            there = (half, tuple(seen), sub)
            sends.append((half, rel, sub, axis, sign, there))
            links.send(t, axis, sign, share(half, sub), there)

        got[half, rel] = got.get((half, rel), 0) + 1
        if sub is None or got[half, rel] == 2:
            last = max([i for i in range(3) if rel[order[i]]], default=-1)
            for i in range(2, last, -1):
                if order[i] == 1:
                    go(1, 1, None)
                else:
                    go(order[i], 1, None)
                    go(order[i], -1, None)
            if last >= 0 and order[last] != 1:
                if rel[order[last]] == 3:
                    go(order[last], 1, 0)
                elif rel[order[last]] == 1:
                    go(order[last], -1, 1)
        plan.append((t, None if rel == (0, 0, 0) else key, sends))
    return plan


def gather_keys():
    plan = gather_plan()
    recv = {step[1]: i for i, step in enumerate(s for s in plan if s[1] is not None)}
    return plan, recv


class Gather:
    def __init__(self, me, own, store, send_sem, recv_sem):
        self.me, self.own, self.store = me, own, store
        self.send_sem, self.recv_sem = send_sem, recv_sem
        self.plan, self.recv = gather_keys()
        self.sent = []

    def copy(self, index, half, rel, sub, axis, sign, there):
        where = span(half, sub)
        here = self.own.at[where] if rel == (0, 0, 0) else self.store.at[slot(self.me, rel), where]
        return pltpu.make_async_remote_copy(
            src_ref=here,
            dst_ref=self.store.at[slot(self.me, rel), where],
            send_sem=self.send_sem.at[index],
            recv_sem=self.recv_sem.at[self.recv[there]],
            device_id=peer(self.me, toward(axis, sign)),
            device_id_type=MESH,
        )

    def arrived(self, key):
        half, rel, sub = key
        here = self.store.at[slot(self.me, rel), span(half, sub)]
        pltpu.make_async_remote_copy(
            src_ref=here,
            dst_ref=here,
            send_sem=self.send_sem.at[0],
            recv_sem=self.recv_sem.at[self.recv[key]],
            device_id=peer(self.me, (1, 0, 0)),
            device_id_type=MESH,
        ).wait_recv()

    def step(self, item):
        _, key, sends = item
        if key is not None:
            self.arrived(key)
        for send in sends:
            self.copy(len(self.sent), *send).start()
            self.sent.append(send)

    def finish(self):
        for index, send in enumerate(self.sent):
            self.copy(index, *send).wait_send()


GROUP = 8
STEPS = 26
PITCH = 4 * IPAD + 3
UNIT_STEPS = 1.6


def transform_kernel(shift, group, part, ctf, txh, tyh, te, to, own, out, store, tx, ty, z1, xs, fr, fi, send_sem, recv_sem, own_sem, tab_sem):
    u = pl.program_id(0)
    me = place()
    work = Gather(me, own, store, send_sem, recv_sem)
    keep = pltpu.make_async_copy(own, store.at[slot(me, (0, 0, 0))], own_sem)
    due = {}
    for item in work.plan:
        at = 0 if item[1] is None else min(STEPS - 1, math.ceil(item[0] * UNIT_STEPS))
        due.setdefault(at, []).append(item)

    loads = [pltpu.make_async_copy(txh, tx, tab_sem.at[0]), pltpu.make_async_copy(tyh, ty, tab_sem.at[1])]

    @pl.when(u == 0)
    def _():
        for load in loads:
            load.start()
        greet(me)
        keep.start()

    for at in sorted(due):
        if at < STEPS - 1:

            @pl.when(u == at)
            def _(at=at):
                for item in due[at]:
                    work.step(item)

    @pl.when(u == 0)
    def _():
        for load in loads:
            load.wait()

    s = jnp.minimum(u, SHIFTS - 1)
    a = s // SIDE
    b = s % SIDE

    @pl.when((b == 0) & (u < SHIFTS))
    def _():
        def ramp(p, carry):
            sx = shift[p, 0] + a - SIDE // 2
            n = jnp.abs(sx)
            sg = jnp.where(sx < 0, -1.0, 1.0).astype(F32)
            for c in range(0, ANGLES, 48):
                rows = pl.ds(c, 48)
                re = part[p, 0, rows, :].astype(F32)
                im = part[p, 1, rows, :].astype(F32)
                co = tx[n, 0, rows, :]
                si = tx[n, 1, rows, :] * sg
                z1[p, 0, rows, :] = re * co + im * si
                z1[p, 1, rows, :] = im * co - re * si
            return carry

        lax.fori_loop(0, GROUP, ramp, 0)

    @pl.when(u < SHIFTS)
    def _():
        for p in range(GROUP):
            sy = shift[p, 1] + b - SIDE // 2
            n = jnp.abs(sy)
            sg = jnp.where(sy < 0, -1.0, 1.0).astype(F32)
            for c in range(0, ANGLES, 16):
                rows = pl.ds(c, 16)
                re = z1[p, 0, rows, :]
                im = z1[p, 1, rows, :]
                co = ty[n, 0, rows, :]
                si = ty[n, 1, rows, :] * sg
                xs[rows, 256 * p : 256 * p + 128] = (re * co + im * si).astype(BF16)
                xs[rows, 256 * p + 128 : 256 * p + 256] = (im * co - re * si).astype(BF16)
        even = jnp.dot(te[...], xs[0:HALF, :], preferred_element_type=F32)
        odd = jnp.dot(to[...], xs[HALF:, :], preferred_element_type=F32)
        for p in range(GROUP):
            j = (u % 2) * GROUP + p
            gain = ctf[pl.ds(group[p], 1), :]
            lo, hi = slice(256 * p, 256 * p + 128), slice(256 * p + 128, 256 * p + 256)
            for c in range(0, IPAD, 8):
                cos, sin = slice(c, c + 8), slice(IPAD + c, IPAD + c + 8)
                er, ei, fr_, fi_ = even[cos, lo], even[cos, hi], even[sin, lo], even[sin, hi]
                gr, gi, hr, hi_ = odd[cos, lo], odd[cos, hi], odd[sin, lo], odd[sin, hi]
                if c == 0:
                    for at, re, im in (
                        (0, fr_[0:1] + hi_[0:1], fi_[0:1] - hr[0:1]),
                        (1, fr_[0:1] - hi_[0:1], fi_[0:1] + hr[0:1]),
                    ):
                        fr[pl.ds(j * PITCH + 4 * IPAD + at, 1), :] = re * gain
                        fi[pl.ds(j * PITCH + 4 * IPAD + at, 1), :] = im * gain
                    rest = lax.broadcasted_iota(jnp.int32, (8, 128), 0) > 0
                    fr_, fi_, hr, hi_ = [jnp.where(rest, v, 0.0) for v in (fr_, fi_, hr, hi_)]
                u1 = (er + fi_) * gain
                u2 = (er - fi_) * gain
                w1 = (ei - fr_) * gain
                w2 = (ei + fr_) * gain
                v1 = (gr + hi_) * gain
                v2 = (gr - hi_) * gain
                y1 = (gi - hr) * gain
                y2 = (gi + hr) * gain
                for blk, (re, im) in enumerate(
                    ((u1 + v1, w1 + y1), (u1 - v1, w1 - y1), (u2 - v2, w2 - y2), (u2 + v2, w2 + y2))
                ):
                    rows = pl.ds(j * PITCH + blk * IPAD + c, 8)
                    fr[rows, :] = re
                    fi[rows, :] = im

    def emit(i, blk, m):
        rows = pl.ds(blk * IPAD + i, 2 * GROUP, stride=PITCH)
        out[m, :, 0:128] = fr[rows, :].astype(BF16)
        out[m, :, 128:256] = fi[rows, :].astype(BF16)

    @pl.when(u % 2 == 1)
    def _():
        def pack(i, carry):
            emit(i, 0, i)
            emit(i, 1, HALF + i)
            emit(i, 2, HALF - i)
            emit(i, 3, ANGLES - i)
            return carry

        emit(0, 0, 0)
        emit(0, 1, HALF)
        emit(0, 4, IPAD)
        emit(1, 4, HALF + IPAD)
        lax.fori_loop(1, HALF // 2, pack, 0, unroll=8)

    @pl.when(u == STEPS - 1)
    def _():
        for item in due.get(STEPS - 1, []):
            work.step(item)
        keep.wait()
        work.finish()


def transform(shift, group, part, ctf, own):
    tx, ty = phase_tables()
    te, to = dft_tables()
    plan, recv = gather_keys()
    whole = pl.BlockSpec(memory_space=pltpu.VMEM)
    near = pl.BlockSpec(memory_space=pltpu.SMEM)
    far = pl.BlockSpec(memory_space=pl.ANY)
    owners = SIZES[0] * SIZES[1] * SIZES[2]
    return pl.pallas_call(
        transform_kernel,
        grid=(STEPS,),
        out_shape=(
            jax.ShapeDtypeStruct((ANGLES, QROWS, 256), BF16),
            jax.ShapeDtypeStruct((owners,) + own.shape, own.dtype),
        ),
        in_specs=[near, near, whole, whole, far, far, whole, whole, whole],
        out_specs=(
            pl.BlockSpec((ANGLES, 2 * GROUP, 256), lambda u: (0, u // 2, 0)),
            pl.BlockSpec(memory_space=pl.ANY),
        ),
        scratch_shapes=[
            pltpu.VMEM((REACH + 1, 2, ANGLES, 128), F32),
            pltpu.VMEM((REACH + 1, 2, ANGLES, 128), F32),
            pltpu.VMEM((GROUP, 2, ANGLES, 128), F32),
            pltpu.VMEM((ANGLES, 256 * GROUP), BF16),
            pltpu.VMEM((2 * GROUP * PITCH + 8, 128), F32),
            pltpu.VMEM((2 * GROUP * PITCH + 8, 128), F32),
            pltpu.SemaphoreType.DMA((sum(len(s[2]) for s in plan),)),
            pltpu.SemaphoreType.DMA((len(recv),)),
            pltpu.SemaphoreType.DMA,
            pltpu.SemaphoreType.DMA((2,)),
        ],
        compiler_params=pltpu.CompilerParams(
            collective_id=1, has_side_effects=True, vmem_limit_bytes=56 * 2**20
        ),
        name="transform",
    )(shift, group, part, ctf, jnp.asarray(tx), jnp.asarray(ty), jnp.asarray(te, BF16), jnp.asarray(to, BF16), own)


H = FOLD // 2
HALF_ROWS = TILES * 8

def fold_of(r):
    return (r, 1) if r <= ROTS // 2 else (ROTS - r, -1)

def half_sums(parts, tab, k):
    even = parts[0] * tab[k, 0:1, :]
    for g in range(2, FOLD, 2):
        even = even + parts[g] * tab[k, g : g + 1, :]
    odd = parts[1] * tab[k, 1:2, :]
    for g in range(3, FOLD, 2):
        odd = odd + parts[g] * tab[k, g : g + 1, :]
    return even, odd

def match_kernel(classes, group, wt, refs, ctf, fwd, bwd, spec, peak, mass, post, acc, power, flat):
    d = pl.program_id(0)
    first = d == 0
    for o in range(4):
        flat[o, 0 : TILES * 16] = refs[o].reshape(TILES * 16, 128).astype(F32)

    def image(r, part):
        at = part * HALF_ROWS + (r % 9) * classes
        return flat[r // 9, pl.ds(at, CPAD), :]

    def product(r, squares):
        re, im = image(r, 0), image(r, 1)
        squares.append(re * re + im * im)
        re, im = re.astype(BF16), im.astype(BF16)
        if fold_of(r)[1] > 0:
            table = jnp.concatenate([jnp.concatenate([re, im], 1), jnp.concatenate([-im, re], 1)], 0)
        else:
            table = jnp.concatenate([jnp.concatenate([re, im], 1), jnp.concatenate([im, -re], 1)], 0)
        return lax.dot_general(wt[r], table, (((1,), (1,)), ((), ())), preferred_element_type=F32)

    @pl.when(first)
    def _():
        acc[...] = jnp.zeros_like(acc)
        power[...] = jnp.zeros_like(power)
        flat[:, TILES * 16 :] = jnp.zeros((4, 8, 128), F32)

    pw = power[...]
    for g in range(FOLD):
        squares = []
        y = product(g, squares)
        if 0 < g < FOLD - 1:
            y = y + product(ROTS - g, squares)
        acc[g] += y
        for term in squares:
            pw = pw + term
    power[...] = pw

    @pl.when(d == pl.num_programs(0) - 1)
    def _():
        gain = jnp.concatenate([ctf[pl.ds(group[p], 1), :] for p in range(8)], 0)
        half = lax.dot_general(
            gain * gain,
            power[...],
            (((1,), (1,)), ((), ())),
            precision=lax.Precision.HIGHEST,
            preferred_element_type=F32,
        ) * (0.5 / ANGLES)
        bias = jnp.concatenate([half, half], 1)
        lane = lax.broadcasted_iota(jnp.int32, (8, 128), 1)
        live = lane % CPAD < classes
        edge = lane < classes
        sign = jnp.where(lane < CPAD, 1.0, -1.0).astype(F32)
        low = -1e30

        def score(s, top):
            rows = pl.ds(pl.multiple_of(s * 8, 8), 8)
            parts = [acc[g, rows, :] for g in range(FOLD)]
            for k in range(H + 1):
                even, odd = half_sums(parts, fwd, k)
                y, w = even + odd, even - odd
                both = [(k, y * sign + pltpu.roll(y, CPAD, 1))]
                if k < H:
                    both.append((FOLD - 1 - k, w + pltpu.roll(w * sign, CPAD, 1)))
                for at, z in both:
                    z = z - bias
                    z = jnp.where(edge if at in (0, FOLD - 1) else live, z, low)
                    spec[at, rows, :] = z
                    top = jnp.maximum(top, z)
            return top

        top = lax.fori_loop(0, SHIFTS, score, jnp.full((8, 128), low, F32), unroll=5)
        top = jnp.max(top, axis=1, keepdims=True)

        def weigh(s, total):
            rows = pl.ds(pl.multiple_of(s * 8, 8), 8)
            parts = []
            for k in range(FOLD):
                e = jnp.exp(spec[k, rows, :] - top)
                total = total + e
                parts.append(e * sign + pltpu.roll(e, CPAD, 1))
            for g in range(H + 1):
                even, odd = half_sums(parts, bwd, g)
                spec[g, rows, :] = even + odd
                if g < H:
                    spec[FOLD - 1 - g, rows, :] = (even - odd) * sign
            return total

        total = lax.fori_loop(0, SHIFTS, weigh, jnp.zeros((8, 128), F32), unroll=5)
        spec[:, SHIFTS * 8 :, :] = jnp.zeros((FOLD, QROWS - SHIFTS * 8, 128), F32)
        peak[...] = jnp.broadcast_to(top, (8, 128))
        mass[...] = jnp.broadcast_to(jnp.sum(total, axis=1, keepdims=True), (8, 128))
        post[...] = total + pltpu.roll(total, CPAD, 1)

def match(group, wt, refs, ctf, classes):
    fwd, bwd = rotation_coefs()
    small = jax.ShapeDtypeStruct((8, 128), F32)
    whole = pl.BlockSpec(memory_space=pltpu.VMEM)
    return pl.pallas_call(
        functools.partial(match_kernel, classes),
        grid=(ANGLES // ROTS,),
        out_shape=(jax.ShapeDtypeStruct((FOLD, QROWS, 128), F32), small, small, small),
        in_specs=[pl.BlockSpec(memory_space=pltpu.SMEM), pl.BlockSpec((ROTS, QROWS, 256), lambda d: (d, 0, 0)),
                  pl.BlockSpec((4, TILES, 16, 128), lambda d: (d, 0, 0, 0)), whole, whole, whole],
        out_specs=(whole,) * 4,
        scratch_shapes=[pltpu.VMEM((FOLD, QROWS, 128), F32), pltpu.VMEM((CPAD, 128), F32), pltpu.VMEM((4, TILES * 16 + 8, 128), F32)],
        compiler_params=pltpu.CompilerParams(vmem_limit_bytes=48 * 2**20),
        name="match",
    )(group, wt, refs, ctf, jnp.asarray(fwd), jnp.asarray(bwd))

COMBOS = [(ry, c) for ry in (1, 0) for c in (2, 1, 3, 0)]
BLOCKS = [(2, 1), (2, 0), (1, 1), (3, 1), (1, 0), (3, 0), (0, 1), (0, 0)]
BLOCK_UNITS = 1.2


def scatter_plan():
    links, steps, got, done = Links(), [], set(), set()

    def send(t, half, stage, combo, kind):
        axis = axes_of(half)[::-1][stage]
        sign = 1 if kind in ("a0", "l0", "l1", "y") else -1
        size = share(half, None if kind == "y" else int(kind[1]))
        msg = (half, stage, combo, kind)
        steps.append((t, "send", msg))
        links.send(t, axis, sign, size, msg)

    def have(half, stage, combo, k):
        if stage == 2:
            return (half, 2, k) in done
        return ((k, combo[0]) if half == 0 else (combo[1], combo[0])) in done

    def ready(t, half, stage, combo, k):
        if k == 2:
            send(t, half, stage, combo, "a0")
            send(t, half, stage, combo, "a1")
        elif k == 1:
            send(t, half, stage, combo, "l1")
            relay(t, half, stage, combo, "a0")
        elif k == 3:
            send(t, half, stage, combo, "r0")
            relay(t, half, stage, combo, "a1")
        else:
            total(t, half, stage, combo)

    def relay(t, half, stage, combo, kind):
        k = 1 if kind == "a0" else 3
        if (half, stage, combo, kind) in got and have(half, stage, combo, k):
            steps.append((t, "relay", (half, stage, combo, kind)))
            send(t, half, stage, combo, "l0" if kind == "a0" else "r1")

    def total(t, half, stage, combo):
        kinds = ("l0", "l1", "r0", "r1")
        if all((half, stage, combo, kind) in got for kind in kinds) and have(half, stage, combo, 0):
            steps.append((t, "total", (half, stage, combo)))
            if stage == 0:
                done.add((half, 0, combo, "s"))
                if combo[0] == 1:
                    send(t, half, 1, combo[1], "y")
                else:
                    second(t, half, combo[1])

    def second(t, half, c):
        if (half, 0, (0, c), "s") in done and (half, 1, c, "y") in got:
            steps.append((t, "pair", (half, c)))
            done.add((half, 2, c))
            ready(t, half, 2, None, c)

    for i, block in enumerate(BLOCKS):
        links.push((i + 1) * BLOCK_UNITS, ("block", block))
    while links.heap:
        t, key = links.pop()
        if key[0] == "block":
            z, y = key[1]
            done.add((z, y))
            for x in (2, 1, 3, 0):
                ready(t, 0, 0, (y, x), z)
                ready(t, 1, 0, (y, z), x)
            continue
        half, stage, combo, kind = key
        steps.append((t, "wait", key))
        got.add(key)
        if kind == "y":
            second(t, half, combo)
        elif kind in ("a0", "a1"):
            relay(t, half, stage, combo, kind)
        else:
            total(t, half, stage, combo)
    return steps


def scatter_keys():
    steps = scatter_plan()
    return steps, {s[2]: i for i, s in enumerate(s for s in steps if s[1] == "send")}


def inner(half, sub):
    low, mid, high = PARTS[half]
    first, end = ((low, high), (low, mid), (mid, high))[0 if sub is None else sub + 1]
    return pl.ds(first - low, end - first)


class Scatter:
    def __init__(self, me, own, three, pair, out, send_sem, recv_sem):
        self.me, self.own, self.three, self.pair, self.out = me, own, three, pair, out
        self.send_sem, self.recv_sem = send_sem, recv_sem
        self.steps, self.index = scatter_keys()
        self.sent = []

    def group(self, stage, combo):
        return 8 if stage == 2 else COMBOS.index(combo)

    def mine(self, half, stage, combo, k, sub=None):
        if stage == 2:
            return self.pair.at[half, k, inner(half, sub)]
        order = axes_of(half)[::-1]
        rel = [0, 0, 0]
        rel[order[0]] = k
        rel[1] = combo[0]
        rel[order[2]] = combo[1]
        return self.own.at[slot(self.me, rel), span(half, sub)]

    def box(self, msg):
        half, stage, combo, kind = msg
        if kind == "y":
            return self.pair.at[half, combo, inner(half, None)]
        which = {"a": 0, "l": 1, "r": 2}[kind[0]]
        return self.three.at[half, self.group(stage, combo), which, inner(half, int(kind[1]))]

    def source(self, msg):
        half, stage, combo, kind = msg
        if kind == "y":
            return self.three.at[half, self.group(0, (1, combo)), 1, inner(half, None)]
        sub = int(kind[1])
        if kind in ("a0", "a1"):
            return self.mine(half, stage, combo, 2, sub)
        if kind == "l1":
            return self.mine(half, stage, combo, 1, sub)
        if kind == "r0":
            return self.mine(half, stage, combo, 3, sub)
        return self.three.at[half, self.group(stage, combo), 0, inner(half, sub)]

    def copy(self, msg, src=None):
        half, stage, combo, kind = msg
        axis = axes_of(half)[::-1][stage]
        sign = 1 if kind in ("a0", "l0", "l1", "y") else -1
        i = self.index[msg]
        box = self.box(msg)
        return pltpu.make_async_remote_copy(
            src_ref=box if src is None else src,
            dst_ref=box,
            send_sem=self.send_sem.at[i],
            recv_sem=self.recv_sem.at[i],
            device_id=peer(self.me, toward(axis, sign)),
            device_id_type=MESH,
        )

    def add(self, dst, terms, count):
        value = terms[0][0:count].astype(F32)
        for term in terms[1:]:
            value = value + term[0:count].astype(F32)
        dst[0:count] = value.astype(dst.dtype)

    def step(self, item):
        _, what, key = item
        if what == "send":
            self.copy(key, self.source(key)).start()
            self.sent.append(key)
        elif what == "wait":
            self.copy(key).wait_recv()
        elif what == "relay":
            half, stage, combo, kind = key
            box = self.box(key)
            sub = int(kind[1])
            mine = self.mine(half, stage, combo, 1 if kind == "a0" else 3, sub)
            self.add(box, (mine, box), inner(half, sub).size)
        elif what == "pair":
            half, c = key
            box = self.pair.at[half, c]
            self.add(box, (self.three.at[half, self.group(0, (0, c)), 1], box), inner(half, None).size)
        else:
            half, stage, combo = key
            left = self.three.at[half, self.group(stage, combo), 1]
            right = self.three.at[half, self.group(stage, combo), 2]
            mine = self.mine(half, stage, combo, 0)
            dst = self.out.at[span(half, None)] if stage == 2 else left
            self.add(dst, (mine, left, right), inner(half, None).size)

    def finish(self):
        for key in self.sent:
            self.copy(key, self.source(key)).wait_send()


def back_kernel(classes, wt, spec, stat, out, logz, own, three, pair, tab, flat, seen, send_sem, recv_sem, stat_send, stat_recv):
    i = pl.program_id(0)
    me = place()
    x, y, z, cls = me
    work = Scatter(me, own, three, pair, out, send_sem, recv_sem)
    last = len(BLOCKS) - 1
    due = {}
    for item in work.steps:
        at = min(last, max(0, math.ceil(item[0] / BLOCK_UNITS - 0.001) - 1))
        due.setdefault(at, []).append(item)

    @pl.when(i == 0)
    def _():
        dp = slot(me, (0, 0, 0))
        barrier = pltpu.get_barrier_semaphore()
        there = [peer(me, toward(*move)) for move in ((0, 1), (0, -1), (1, 1), (2, 1), (2, -1))]
        others = [(dp, (cls + k) % 4) for k in (1, 2, 3)]
        for device in there + others:
            pl.semaphore_signal(barrier, inc=1, device_id=device, device_id_type=MESH)
        pl.semaphore_wait(barrier, len(there) + len(others))
        copies = []
        for k, device in enumerate(others):
            copy = pltpu.make_async_remote_copy(
                src_ref=stat,
                dst_ref=seen.at[k],
                send_sem=stat_send.at[k],
                recv_sem=stat_recv.at[k],
                device_id=device,
                device_id_type=MESH,
            )
            copy.start()
            copies.append(copy)
        for copy in copies:
            copy.wait()
        peaks = [stat[0]] + [seen[k, 0] for k in range(3)]
        masses = [stat[1]] + [seen[k, 1] for k in range(3)]
        top = jnp.maximum(jnp.maximum(peaks[0], peaks[1]), jnp.maximum(peaks[2], peaks[3]))
        mass = masses[0] * jnp.exp(peaks[0] - top)
        for k in range(1, 4):
            mass = mass + masses[k] * jnp.exp(peaks[k] - top)
        total = top + jnp.log(mass)
        logz[...] = total
        scale = jnp.concatenate([jnp.exp(peaks[0] - total)] * (QROWS // 8), 0)
        for g in range(FOLD):
            tab[g] = (spec[g] * scale).T.astype(BF16)

    dz = jnp.int32(0)
    dy = jnp.int32(0)
    for at, (bz, by) in enumerate(BLOCKS):
        dz = jnp.where(i == at, bz, dz)
        dy = jnp.where(i == at, by, dy)
    base = (((z + dz) % 4) * 2 + (y + dy) % 2) * 4
    for o in range(4):
        for j in range(9):
            g, sg = fold_of(o * 9 + j)
            both = jnp.dot(tab[g], wt[o * 9 + j], preferred_element_type=F32)
            a, b = both[:CPAD], both[CPAD:]
            rows = CPAD if j < 8 else HALF_ROWS - 8 * classes
            flat[o, 0, pl.ds(j * classes, rows), :] = (a[:, :128] - sg * b[:, 128:])[:rows]
            flat[o, 1, pl.ds(j * classes, rows), :] = (a[:, 128:] + sg * b[:, :128])[:rows]
        own[base + o] = flat[o].astype(BF16).reshape(TILES, 16, 128)

    for at in range(len(BLOCKS)):

        @pl.when(i == at)
        def _(at=at):
            for item in due.get(at, []):
                work.step(item)
            if at == last:
                work.finish()


def block_index(i):
    dp = lax.axis_index("dp")
    dz = jnp.int32(0)
    dy = jnp.int32(0)
    for at, (bz, by) in enumerate(BLOCKS):
        dz = jnp.where(i == at, bz, dz)
        dy = jnp.where(i == at, by, dy)
    return ((dp // 8 + dz) % 4) * 2 + ((dp // 4) % 2 + dy) % 2, 0, 0


def back(wt, spec, stat, classes):
    steps, index = scatter_keys()
    whole = pl.BlockSpec(memory_space=pltpu.VMEM)
    owners = SIZES[0] * SIZES[1] * SIZES[2]
    half = (TILES // 2 + 1, 16, 128)
    return pl.pallas_call(
        functools.partial(back_kernel, classes),
        grid=(len(BLOCKS),),
        out_shape=(jax.ShapeDtypeStruct((TILES, 16, 128), F32), jax.ShapeDtypeStruct((8, 128), F32)),
        in_specs=[pl.BlockSpec((ROTS, QROWS, 256), block_index), whole, whole],
        out_specs=(whole, whole),
        scratch_shapes=[
            pltpu.VMEM((owners, TILES, 16, 128), BF16),
            pltpu.VMEM((2, 9, 3) + half, BF16),
            pltpu.VMEM((2, 4) + half, BF16),
            pltpu.VMEM((FOLD, 128, QROWS), BF16),
            pltpu.VMEM((4, 2, HALF_ROWS, 128), F32),
            pltpu.VMEM((3, 2, 8, 128), F32),
            pltpu.SemaphoreType.DMA((len(index),)),
            pltpu.SemaphoreType.DMA((len(index),)),
            pltpu.SemaphoreType.DMA((3,)),
            pltpu.SemaphoreType.DMA((3,)),
        ],
        compiler_params=pltpu.CompilerParams(
            collective_id=2, has_side_effects=True, vmem_limit_bytes=48 * 2**20
        ),
        name="back",
    )(wt, spec, stat)


def twist_tables(freq, rot_offset):
    idx = (freq[:, None] * rot_offset[None, :]) % ANGLES
    rad = idx.astype(F32) * (2.0 * math.pi / ANGLES)
    return jnp.cos(rad)[:, :, None], jnp.sin(rad)[:, :, None]


def twist_refs(references, cos, sin):
    re = references[:, 0].astype(F32)
    im = references[:, 1].astype(F32)
    both = jnp.stack([re * cos + im * sin, im * cos - re * sin], 0).astype(BF16)
    both = both.reshape(2, -1, both.shape[3])
    both = jnp.pad(both, ((0, 0), (0, HALF_ROWS - both.shape[1]), (0, 0)))
    return both.reshape(TILES, 16, both.shape[2])


def untwist(sums, cos, sin, block, classes):
    rows = sums.reshape(2, HALF_ROWS, -1)[:, : block * classes].reshape(2, block, classes, -1)
    re, im = rows[0], rows[1]
    return jnp.stack([re * cos - im * sin, re * sin + im * cos], 1)


def order_angles(particles):
    return jnp.concatenate([particles[:, :, 0::2], particles[:, :, 1::2]], 2)


def local(particles, references, ctf_table, rot_offset, prior_shift, defocus_group):
    block, _, classes = references.shape[:3]
    freq = lax.axis_index("dp") * block + jnp.arange(block, dtype=jnp.int32)
    cos, sin = twist_tables(freq, rot_offset)
    wt, refs = transform(
        prior_shift, defocus_group, order_angles(particles), ctf_table, twist_refs(references, cos, sin)
    )
    spec, peak, mass, post = match(defocus_group, wt, refs, ctf_table, classes)
    sums, total = back(wt, spec, jnp.stack([peak, mass]), classes)
    posterior = post[:, :classes] * jnp.exp(peak[:, :classes] - total[:, :classes])
    return total[:, 0], posterior, untwist(sums, cos, sin, block, classes)


def solution(mesh):
    placed = (
        P("dp", None, None, None),
        P("dp", None, "cls", None),
        P(),
        P("cls"),
        P("dp", None),
        P("dp"),
    )
    return jax.shard_map(
        local,
        mesh=mesh,
        in_specs=placed,
        out_specs=(P("dp"), P("dp", "cls"), P("dp", None, "cls", None)),
        check_vma=False,
    )
```
